128 devices in a mesh: cells: 128 (over z, y, x, core).
Axes of the slice: x: 4, y: 4, z: 4, core: 2. Of those that a mesh axis runs over, the one named last changes fastest.
Arguments:
- positions: float32 [3, 1048576], P(None, 'cells'), may hold values from 0 to 1
- velocities: float32 [3, 1048576], P(None, 'cells'), may hold values from -6 to 6
- masses: float32 [1048576], P('cells'), may hold values from 0.5 to 2
- smoothing: float32 [1048576], P('cells'), may hold values from 0.5 to 1
- energies: float32 [1048576], P('cells'), may hold values from 0.5 to 2
- cell_counts: int32 [4096], P('cells'), may hold values from 128 to 256, as said below
- pair_list: int32 [4, 16384], P(None, 'cells'), may hold values from 0 to 31, as said below
- export_list: int32 [128, 26, 8], P('cells'), may hold values from -1 to 31, as said below
- mesh_owner: int32 [1048576, 1], P('cells'), may hold values from 0 to 127; in each aligned block of 8192 rows (0 to 8191, 8192 to 16383, ...) at most 128 rows name the same one
- mesh_cell: int32 [1048576], P('cells'), may hold values from 0 to 131071
Outputs:
- density: float32 [1048576], P('cells')
- acceleration: float32 [3, 1048576], P(None, 'cells')
- heating: float32 [1048576], P('cells')
- potential: float32 [256, 256, 256], P('cells')
The draws below stay inside these ranges and needn't reach their ends.
Inputs may be any that keep to these rules, and one draw needn't show every extreme that they name: `cell_counts`: slots at and beyond a cell's count are padding; every device has at least one cell with all 256 slots live. `pair_list`: row 0 is the owner cell's index on the listing device, row 1 a neighbour index of 0 to 25, row 2 a slot of 0 to 7, row 3 a neighbour direction of 0 to 26 other than 13. Every device lists exactly 128 cross pairs, each (neighbour index, slot) at most once, at most 8 with one neighbour index and exactly 8 with one of them. `export_list`: entry [f, j, t] is the cell of device f that the device whose pair with neighbour index j and slot t names device f reads, or -1 where no pair names that slot. `mesh_owner`: at most 128 particles of one device have their mesh cell in one device's planes.
All inputs are finite; a program needn't handle non-finite values.
Results may differ from the reference program's by a relative error of at most 0.0003.
Values sent between devices are 32-bit elements; how exact they have to be, the bound alone decides.
No kernel may reach another device: no remote copies, remote signals or barrier semaphores. Data moves between devices by JAX's collectives and lax.ppermute only.
A program may use at most 64 MiB of HBM per device.

```python
import math
import jax
import jax.numpy as jnp
import numpy as np
from jax import lax

CELLS_DEV = 32
P_SIZE = 256
PAIRS_DEV = 128
PEERS = 26
M = 256
CAP = 8
GCAP = 128
SLAB = 2
NCELL = 4096
NPART = 1048576
N_CELLS = 128


def pair_tables(key):
    key_hot, key_order, key_owner, key_cell, key_way = jax.random.split(key, 5)
    hot_device = jax.random.randint(key_hot, (), 0, N_CELLS, dtype=jnp.int32)
    devices = jnp.arange(N_CELLS, dtype=jnp.int32)
    half_peers = PEERS // 2
    peer_iota = jnp.arange(PEERS, dtype=jnp.int32)
    step_along = jnp.where(peer_iota < half_peers, peer_iota - half_peers, peer_iota - half_peers + 1).astype(jnp.int32)
    slots_all = jnp.arange(PAIRS_DEV, dtype=jnp.int32)

    def per_device(device, subkey):
        key_pick, key_perm = jax.random.split(subkey)
        apart = (hot_device - device) % N_CELLS
        apart = jnp.where(apart >= N_CELLS // 2, apart - N_CELLS, apart)
        nearby = (apart != 0) & (jnp.abs(apart) <= half_peers)
        near_index = jnp.where(apart < 0, apart + half_peers, apart + half_peers - 1)
        random_index = jax.random.randint(key_pick, (), 0, PEERS, dtype=jnp.int32)
        heavy = jnp.where(nearby, near_index, random_index).astype(jnp.int32)
        scores = jax.random.permutation(key_perm, PEERS).astype(jnp.int32)
        scores = jnp.where(peer_iota == heavy, PEERS, scores)
        ordering = jnp.argsort(scores, stable=True).astype(jnp.int32)
        to_heavy = slots_all < CAP
        remaining = jnp.maximum(slots_all - CAP, 0)
        neighbour = jnp.where(to_heavy, heavy, ordering[remaining % (PEERS - 1)])
        places = jnp.where(to_heavy, slots_all, remaining // (PEERS - 1))
        return (neighbour.astype(jnp.int32), places.astype(jnp.int32))
    neighbour, places = jax.vmap(per_device)(devices, jax.random.split(key_order, N_CELLS))
    owners = jax.random.randint(key_owner, (N_CELLS, PAIRS_DEV), 0, CELLS_DEV, dtype=jnp.int32)
    foreign = jax.random.randint(key_cell, (N_CELLS, PAIRS_DEV), 0, CELLS_DEV, dtype=jnp.int32)
    directions = jax.random.randint(key_way, (N_CELLS, PAIRS_DEV), 0, 26, dtype=jnp.int32)
    directions = directions + (directions >= 13).astype(jnp.int32)
    sender_rows = (devices[:, None] + step_along[neighbour]) % N_CELLS
    export_table = jnp.full((N_CELLS, PEERS, CAP), -1, jnp.int32).at[sender_rows, neighbour, places].set(foreign)
    pair_table = jnp.stack([owners, neighbour, places, directions]).reshape(4, N_CELLS * PAIRS_DEV)
    return (pair_table, export_table)


def draw_pair_list(key, part):
    pair_table, export_table = pair_tables(key)
    return pair_table


def draw_export_list(key, part):
    pair_table, export_table = pair_tables(key)
    return export_table


def draw_cell_counts(key, part):
    key = jax.random.fold_in(key, 7)
    key_count, key_full = jax.random.split(key)
    counts = jax.random.randint(key_count, (NCELL,), P_SIZE // 2, P_SIZE + 1, dtype=jnp.int32)
    full_cells = jax.random.randint(key_full, (N_CELLS,), 0, CELLS_DEV, dtype=jnp.int32) + jnp.arange(N_CELLS, dtype=jnp.int32) * CELLS_DEV
    return counts.at[full_cells].set(P_SIZE)


def place_ends(drawn, own_key, least, largest):
    extent = drawn.shape
    index_at = [jax.random.randint(jax.random.fold_in(own_key, axis), (), 0, extent[axis]) for axis in range(len(extent))]
    drawn = drawn.at[tuple(index_at)].set(least)
    longest = extent.index(max(extent))
    index_at[longest] = (index_at[longest] + 1) % extent[longest]
    return drawn.at[tuple(index_at)].set(largest)


def block_levels(own_key, shape, shards, smallest, top_value):
    loudness, own = 1.0, jax.random.fold_in(own_key, 6)
    for position, parts in shards:
        draws = jnp.exp(jax.random.uniform(jax.random.fold_in(own, position), (parts,), jnp.float32, smallest / len(shards), top_value / len(shards)))
        loudness = loudness * jnp.repeat(draws, shape[position] // parts).reshape([-1 if axis == position else 1 for axis in range(len(shape))])
    return loudness


def assign_block(stream_key, own, number, rows, amount, top, bound, slope):
    sequence = jax.random.permutation(stream_key, amount)
    heavy_load, usual = portions_of(amount, rows * top, bound, slope, True), portions_of(amount, rows * top, bound, slope, False)
    places = jnp.arange(amount)

    def named(tallies, offset_by):
        used = int((tallies > 0).sum())
        fixed = max(1, used // 4)
        shifted = fixed + (places - fixed + offset_by * (used - fixed)) % max(1, amount - fixed)
        return jnp.zeros((amount,), jnp.int32).at[sequence[jnp.where(places < fixed, places, shifted)]].set(jnp.asarray(tallies, jnp.int32))

    tallies = jnp.where(number % 4 == 0, named(heavy_load, number // 4), named(usual, number - number // 4 - 1))
    mixed = jax.random.permutation(jax.random.fold_in(own, 3), amount)
    donor, receiver = mixed[0:amount // 2 * 2:2], mixed[1:amount // 2 * 2:2]
    margin = jnp.minimum(tallies[donor] - 1, bound - tallies[receiver]) // 2
    margin = jnp.where((donor == sequence[0]) | (receiver == sequence[0]) | (tallies[receiver] == 0), 0, jnp.maximum(margin, 0))
    shifted = jax.random.randint(jax.random.fold_in(own, 4), (amount // 2,), 0, 1 << 20) % (margin + 1)
    tallies = tallies.at[donor].add(-shifted).at[receiver].add(shifted)
    items = jnp.searchsorted(jnp.cumsum(tallies), jnp.arange(rows * top), side="right").astype(jnp.int32)
    table = items.reshape(top, rows).T
    table = table[jax.random.permutation(jax.random.fold_in(own, 1), rows)]
    offset_by = jax.random.randint(jax.random.fold_in(own, 2), (rows, 1), 0, top)
    return jnp.take_along_axis(table, (jnp.arange(top)[None, :] + offset_by) % top, axis=1)


def portions_of(amount, total, limit, lean, full):
    weights = [(1 << 20) // math.isqrt(rank ** lean) + 1 for rank in range(1, amount + 1)]
    largest = limit if full else min(limit, max(-(-total // amount), total * weights[0] // sum(weights)))
    least = 1 if total - largest >= amount - 1 else 0
    given, surplus = [largest] + [least] * (amount - 1), total - largest - least * (amount - 1)
    while surplus > 0:
        movable = [i for i in range(1, amount) if given[i] < largest] or [i for i in range(1, amount) if given[i] < limit]
        whole, left = sum([weights[i] for i in movable]), surplus
        for i in movable:
            more = min(limit - given[i], max(1, left * weights[i] // whole), surplus)
            given[i] = given[i] + more
            surplus = surplus - more
    return np.array(given)


def gaussian(rng, dims, deviation, reach, shards=(), kind=jnp.bfloat16):
    values = deviation * jax.random.normal(rng, dims, jnp.float32)
    if shards:
        values = values * block_levels(rng, dims, shards, -0.22, 0.18)
    return jnp.clip(values, -reach, reach).astype(kind)


def setup_inputs(seed: int = 0) -> dict:
    key_of = jax.random.split(jax.random.key(seed), 11)
    positions = jnp.clip(1.0 * jax.random.uniform(key_of[0], (3, NPART), jnp.float32) ** block_levels(key_of[0], (3, NPART), ((1, 128),), -0.2, 0.2), 0.0, 1.0)
    velocities = gaussian(key_of[1], (3, NPART), 1.0, 6.0, ((1, 128),), jnp.float32)
    masses = jnp.clip(jnp.exp(math.log(2.0) - 1.3862944 * jax.random.uniform(key_of[2], (NPART,), jnp.float32) ** block_levels(key_of[2], (NPART,), ((0, 128),), -0.2, 0.2)), 0.5, 2.0)
    smoothing = jnp.clip(jnp.exp(math.log(1.0) - 0.6931472 * jax.random.uniform(key_of[3], (NPART,), jnp.float32) ** block_levels(key_of[3], (NPART,), ((0, 128),), -0.2, 0.2)), 0.5, 1.0)
    energies = jnp.clip(jnp.exp(math.log(2.0) - 1.3862944 * jax.random.uniform(key_of[4], (NPART,), jnp.float32) ** block_levels(key_of[4], (NPART,), ((0, 128),), -0.2, 0.2)), 0.5, 2.0)
    cell_counts = draw_cell_counts(jax.random.fold_in(key_of[10], 71), 0)
    pair_list = draw_pair_list(jax.random.fold_in(key_of[10], 71), 0)
    export_list = draw_export_list(jax.random.fold_in(key_of[10], 71), 0)
    mesh_owner_keys = jax.random.split(jax.random.fold_in(key_of[8], 1), NPART // (CELLS_DEV * P_SIZE))
    mesh_owner_turns = jax.random.permutation(jax.random.fold_in(key_of[8], 3), NPART // (CELLS_DEV * P_SIZE))
    mesh_owner = jax.vmap(lambda own, number: assign_block(jax.random.fold_in(key_of[8], 2), own, number, CELLS_DEV * P_SIZE, N_CELLS, 1, GCAP, 2))(mesh_owner_keys, mesh_owner_turns).reshape((NPART, 1))
    mesh_cell = place_ends(jax.random.randint(key_of[9], (NPART,), 0, SLAB * M * M), jax.random.fold_in(key_of[9], 1), 0, (SLAB * M * M) - 1).astype(jnp.int32)
    return dict(positions=positions, velocities=velocities, masses=masses, smoothing=smoothing, energies=energies, cell_counts=cell_counts, pair_list=pair_list, export_list=export_list, mesh_owner=mesh_owner, mesh_cell=mesh_cell)


spline_norm = 8.0 / math.pi

def spline_value(scaled_dist):
    inner_part = 1.0 - 6.0 * scaled_dist * scaled_dist + 6.0 * scaled_dist * scaled_dist * scaled_dist
    outer_part = 2.0 * (1.0 - scaled_dist) ** 3
    return jnp.where(scaled_dist <= 0.5, inner_part, jnp.where(scaled_dist <= 1.0, outer_part, 0.0))

def spline_slope(scaled_dist):
    inner_part = -12.0 + 18.0 * scaled_dist
    outer_part = -6.0 * (1.0 - scaled_dist) ** 2 / jnp.maximum(scaled_dist, 0.5)
    return jnp.where(scaled_dist <= 0.5, inner_part, jnp.where(scaled_dist <= 1.0, outer_part, 0.0))

def offsets(direction):
    return jnp.stack([direction // 9 - 1, direction // 3 % 3 - 1, direction % 3 - 1], axis=1).astype(jnp.float32)

def density_terms(own_pos, own_reach, far_pos, far_weight):
    separation = own_pos[:, :, :, None] - far_pos[:, :, None, :]
    distance = jnp.sqrt(lax.optimization_barrier(jnp.sum(separation * separation, axis=1)))
    scaled_dist = distance / own_reach[:, :, None]
    scale_own = spline_norm / own_reach ** 3
    return scale_own * lax.optimization_barrier(jnp.sum(spline_value(scaled_dist) * far_weight[:, None, :], axis=2))

def force_terms(own_pos, own_vel, own_reach, own_factor, far_pos, far_vel, far_reach, far_factor, far_weight):
    separation = own_pos[:, :, :, None] - far_pos[:, :, None, :]
    distance = jnp.sqrt(lax.optimization_barrier(jnp.sum(separation * separation, axis=1)))
    own_slope = spline_norm * spline_slope(distance / own_reach[:, :, None]) / own_reach[:, :, None] ** 5
    far_slope = spline_norm * spline_slope(distance / far_reach[:, None, :]) / far_reach[:, None, :] ** 5
    coefficient = far_weight[:, None, :] * (own_factor[:, :, None] * own_slope + far_factor[:, None, :] * far_slope)
    push = -lax.optimization_barrier(jnp.sum(coefficient[:, None] * separation, axis=3))
    relative = own_vel[:, :, :, None] - far_vel[:, :, None, :]
    closing = lax.optimization_barrier(jnp.sum(relative * separation, axis=1))
    warming = own_factor * lax.optimization_barrier(jnp.sum(far_weight[:, None, :] * own_slope * closing, axis=2))
    return jnp.concatenate([push, warming[:, None, :]], axis=1)

def reference(positions, velocities, masses, smoothing, energies, cell_counts, pair_list, export_list, mesh_owner, mesh_cell):
    ncells = CELLS_DEV * N_CELLS
    slots_iota = jnp.arange(P_SIZE, dtype=jnp.int32)
    live_mask = (slots_iota[None, :] < cell_counts[:, None]).astype(jnp.float32)
    cell_pos = jnp.moveaxis(positions.reshape(3, ncells, P_SIZE), 1, 0)
    cell_vel = jnp.moveaxis(velocities.reshape(3, ncells, P_SIZE), 1, 0)
    weight = masses.reshape(ncells, P_SIZE) * live_mask / P_SIZE
    own_reach = smoothing.reshape(ncells, P_SIZE)
    own_heat = energies.reshape(ncells, P_SIZE)
    pair_table = pair_list.reshape(4, N_CELLS, PAIRS_DEV)
    device_of = jnp.broadcast_to(jnp.arange(N_CELLS, dtype=jnp.int32)[:, None], pair_table[1].shape)
    half_peers = PEERS // 2
    neighbour = pair_table[1]
    step_along = jnp.where(neighbour < half_peers, neighbour - half_peers, neighbour - half_peers + 1).astype(jnp.int32)
    foreign_device = ((device_of + step_along) % N_CELLS).astype(jnp.int32)
    owner_cell = (device_of * CELLS_DEV + pair_table[0]).reshape(-1)
    foreign_local = export_list[foreign_device, neighbour, pair_table[2]]
    foreign_cell = (foreign_device * CELLS_DEV + foreign_local).reshape(-1)
    every_cell = jnp.arange(ncells, dtype=jnp.int32)
    owners = jnp.concatenate([every_cell, owner_cell]).astype(jnp.int32)
    partners = jnp.concatenate([every_cell, foreign_cell]).astype(jnp.int32)
    directions = jnp.concatenate([jnp.full((ncells,), 13, jnp.int32), pair_table[3].reshape(-1)])
    shifts = offsets(directions)
    blocks = owners.shape[0] // N_CELLS
    owner_blocks = owners.reshape(blocks, N_CELLS)
    partner_blocks = partners.reshape(blocks, N_CELLS)
    shift_blocks = shifts.reshape(blocks, N_CELLS, 3)

    def density_block(block_args):
        mine, theirs, moved = block_args
        return density_terms(cell_pos[mine], own_reach[mine], cell_pos[theirs] + moved[:, :, None], weight[theirs])
    density_parts = lax.map(density_block, (owner_blocks, partner_blocks, shift_blocks)).reshape(-1, P_SIZE)
    raw_density = jax.ops.segment_sum(density_parts, owners, num_segments=ncells)
    density = jnp.where(live_mask > 0, raw_density, 1.0)
    factor = 2.0 / 3.0 * own_heat / density

    def force_block(block_args):
        mine, theirs, moved = block_args
        return force_terms(cell_pos[mine], cell_vel[mine], own_reach[mine], factor[mine], cell_pos[theirs] + moved[:, :, None], cell_vel[theirs], own_reach[theirs], factor[theirs], weight[theirs])
    force_parts = lax.map(force_block, (owner_blocks, partner_blocks, shift_blocks)).reshape(-1, 4, P_SIZE)
    summed_force = jax.ops.segment_sum(force_parts, owners, num_segments=ncells) * live_mask[:, None, :]
    acceleration = jnp.moveaxis(summed_force[:, 0:3], 0, 1).reshape(3, -1)
    heating = summed_force[:, 3].reshape(-1)
    slab_cells = M // N_CELLS * M * M
    flat_index = (mesh_owner[:, 0] * slab_cells + mesh_cell).astype(jnp.int32)
    mass_grid = jax.ops.segment_sum(masses * live_mask.reshape(-1), flat_index, num_segments=M * M * M).reshape(M, M, M)
    spectrum = jnp.fft.fftn(mass_grid)
    wave_index = jnp.arange(M, dtype=jnp.int32)
    signed = jnp.where(wave_index < M // 2, wave_index, wave_index - M).astype(jnp.float32)
    wave_step = 2.0 * math.pi / M
    wave_square = wave_step * wave_step * (signed[:, None, None] ** 2 + signed[None, :, None] ** 2 + signed[None, None, :] ** 2)
    green_factor = jnp.where(wave_square > 0, -1.0 / jnp.where(wave_square > 0, wave_square, 1.0), 0.0)
    potential = jnp.real(jnp.fft.ifftn(spectrum * green_factor)).astype(jnp.float32)
    return (density.reshape(-1), acceleration, heating, potential)
```

```python
import functools
import math

import jax
import jax.numpy as jnp
import numpy as np
from jax import lax
from jax.experimental import pallas as pl
from jax.experimental.pallas import tpu as pltpu
from jax.sharding import PartitionSpec as P

M = 256
GROUP = 32
CAP = 8
HALF = 13
CELLS = 32
SLOTS = 256
STRIP = 32
F32 = jnp.float32
BF16 = jnp.bfloat16
NORM = 8.0 / math.pi
TINY = 1e-30
VMEM = pl.BlockSpec(memory_space=pltpu.VMEM)
SMEM = pl.BlockSpec(memory_space=pltpu.SMEM)
NT = (((1,), (1,)), ((), ()))
NN = (((1,), (0,)), ((), ()))
highest = lax.Precision.HIGHEST


def params(mib):
    return pltpu.CompilerParams(vmem_limit_bytes=mib * 1024 * 1024)


def cost(flops, nbytes):
    return pl.CostEstimate(flops=int(flops), bytes_accessed=int(nbytes), transcendentals=0)


def row_index(shape):
    return lax.broadcasted_iota(jnp.int32, shape, 0)


def rounded(value):
    return value.astype(BF16).astype(F32)


def thirds(value):
    first = rounded(value)
    rest = value - first
    second = rounded(rest)
    return first, second, rest - second


def place_rows(block, shift):
    row = row_index(block.shape)
    moved = jnp.where(row == 0, shift[0], jnp.where(row == 1, shift[1], shift[2])) - 0.5
    return row, jnp.where(row < 3, block + moved, 0.0)


def far_stack(basis):
    first, second, third = thirds(basis)
    return jnp.concatenate([first, second, first, second, third, first], axis=0)


def own_stack(basis):
    first, second, third = thirds(basis)
    return jnp.concatenate([first, first, second, second, first, third], axis=0)


def far_basis(block, shift):
    row, place = place_rows(block, shift)
    square = jnp.sum(place * place, axis=0, keepdims=True)
    basis = jnp.where(row == 3, square, jnp.where(row == 4, 1.0, place))
    return row, place, basis


def own_tables(own_ref, table_ref):
    zeros = jnp.zeros((16, SLOTS), F32)

    def one_cell(cell):
        block = own_ref[cell]
        row, place = place_rows(block, (0.0, 0.0, 0.0))
        square = jnp.sum(place * place, axis=0, keepdims=True)
        reach = block[7:8]
        inverse = 1.0 / (reach * reach)
        basis = jnp.where(
            row < 3, -2.0 * place, jnp.where(row == 3, 1.0, jnp.where(row == 4, square, 0.0))
        )
        stacked = jnp.concatenate(
            [own_stack(basis * inverse), zeros, own_stack(basis), zeros], axis=0
        )
        table_ref[cell] = stacked.T.astype(BF16)

    def some_cells(step, carry):
        for part in range(4):
            one_cell(step * 4 + part)
        return carry

    lax.fori_loop(0, CELLS // 4, some_cells, 0)


def kernel_half(square):
    square = jnp.maximum(square, TINY)
    dist = square * lax.rsqrt(square)
    left = jnp.maximum(1.0 - dist, 0.0)
    inner = 0.5 - 3.0 * square * left
    outer = left * left * left
    return jnp.where(square <= 0.25, inner, outer)


def slope_sixth(square):
    square = jnp.minimum(jnp.maximum(square, TINY), 1.0)
    inverse = lax.rsqrt(square)
    dist = square * inverse
    inner = 3.0 * dist - 2.0
    outer = (2.0 - dist) - inverse
    return jnp.where(square <= 0.25, inner, outer)


def in_turn(amount, first_half, second_half):
    first_half(0, 0)

    def two_pairs(step, carry):
        pair = 2 * step
        first_half(pair + 1, 1)
        second_half(pair, 0)
        first_half(jnp.minimum(pair + 2, amount - 1), 0)
        second_half(pair + 1, 1)
        return carry

    lax.fori_loop(0, amount // 2, two_pairs, 0)


def density_first(table_ref, square_ref, owner, block, shift):
    _, _, basis = far_basis(block, shift)
    far = jnp.concatenate([far_stack(basis), jnp.zeros((80, SLOTS), F32)], axis=0).astype(BF16)
    square_ref[...] = lax.dot_general(table_ref[owner], far, NN, preferred_element_type=F32)


def density_second(total_ref, square_ref, owner, weight):
    for start in range(0, SLOTS, STRIP):
        terms = kernel_half(square_ref[start : start + STRIP, :]) * weight
        total_ref[owner, start : start + STRIP, :] += terms[:, 0:128] + terms[:, 128:256]


def listed(which, info_ref, list_ref):
    pairs = info_ref.shape[1]

    def one_pair(pair, found):
        list_ref[found] = pair
        return found + (info_ref[2, pair] == which).astype(jnp.int32)

    found = lax.fori_loop(0, pairs, one_pair, jnp.int32(0))
    list_ref[found] = pairs
    list_ref[found + 1] = pairs
    return (found + 1) // 2 * 2


def pair_at(list_ref, info_ref, shift_ref, place):
    pair = list_ref[place]
    real = pair < info_ref.shape[1]
    pair = jnp.minimum(pair, info_ref.shape[1] - 1)
    owner = info_ref[0, pair]
    shift = (shift_ref[0, pair], shift_ref[1, pair], shift_ref[2, pair])
    return owner, jnp.where(real, owner, CELLS), info_ref[1, pair], shift


NO_SHIFT = (0.0, 0.0, 0.0)


def density_self_kernel(own_ref, table_ref, total_ref, even_ref, odd_ref):
    own_tables(own_ref, table_ref)
    total_ref[...] = jnp.zeros_like(total_ref)
    buffers = (even_ref, odd_ref)

    def first_half(cell, buffer):
        density_first(table_ref, buffers[buffer], cell, own_ref[cell], NO_SHIFT)

    def second_half(cell, buffer):
        density_second(total_ref, buffers[buffer], cell, own_ref[cell, 3:4, :])

    in_turn(CELLS, first_half, second_half)


def density_cross_kernel(which, finish, count_ref, info_ref, shift_ref, table_ref, far_ref, *refs):
    if finish:
        own_ref, heat_ref, before_ref, total_ref, density_ref, factor_ref = refs[:6]
    else:
        before_ref, total_ref = refs[:2]
    list_ref, even_ref, odd_ref = refs[-3:]
    buffers = (even_ref, odd_ref)
    amount = listed(which, info_ref, list_ref)

    def first_half(place, buffer):
        owner, _, source, shift = pair_at(list_ref, info_ref, shift_ref, place)
        density_first(table_ref, buffers[buffer], owner, far_ref[source], shift)

    def second_half(place, buffer):
        _, target, source, _ = pair_at(list_ref, info_ref, shift_ref, place)
        density_second(total_ref, buffers[buffer], target, far_ref[source, 3:4, :])

    in_turn(amount, first_half, second_half)
    if not finish:
        return

    lane = lax.broadcasted_iota(jnp.int32, (1, SLOTS), 1)

    def one_cell(cell):
        raw = jnp.sum(total_ref[cell].T, axis=0, keepdims=True)
        reach = own_ref[cell, 7:8, :]
        raw = raw * (2.0 * NORM) / (reach * reach * reach)
        density = jnp.where(lane < count_ref[cell], raw, 1.0)
        density_ref[pl.ds(cell, 1), :] = density
        factor_ref[pl.ds(cell, 1), :] = 2.0 / 3.0 * heat_ref[pl.ds(cell, 1), :] / density

    def some_cells(step, carry):
        for part in range(4):
            one_cell(step * 4 + part)
        return carry

    lax.fori_loop(0, CELLS // 4, some_cells, 0)


def force_first(table_ref, own_square_ref, far_square_ref, column_ref, owner, block, factor, shift):
    row, place, basis = far_basis(block, shift)
    reach = block[7:8]
    weight = block[3:4]
    inverse = 1.0 / (reach * reach)
    pad_low = jnp.zeros((80, SLOTS), F32)
    pad_high = jnp.zeros((64, SLOTS), F32)
    pad_end = jnp.zeros((16, SLOTS), F32)
    far_own = jnp.concatenate([far_stack(basis), pad_low], axis=0).astype(BF16)
    far_far = jnp.concatenate([pad_high, far_stack(basis * inverse), pad_end], axis=0).astype(BF16)
    table = table_ref[owner]
    own_square_ref[...] = lax.dot_general(table, far_own, NN, preferred_element_type=F32)
    far_square_ref[...] = lax.dot_general(table, far_far, NN, preferred_element_type=F32)
    swirl = jnp.sum(place[0:3] * block[4:7], axis=0, keepdims=True)
    own_side = jnp.where(
        row < 3, place, jnp.where(row == 3, 1.0, jnp.where(row == 7, swirl, block))
    )
    own_side = own_side * weight
    far_side = jnp.where(row < 3, place, jnp.where(row == 3, 1.0, 0.0))
    far_side = far_side * (weight * factor * (6.0 * NORM) * inverse * inverse / reach)
    own_first = rounded(own_side)
    own_second = own_side - own_first
    far_first = rounded(far_side)
    far_second = far_side - far_first
    none = jnp.zeros((8, SLOTS), F32)
    column_ref[...] = jnp.concatenate(
        [
            jnp.concatenate([own_first, own_second, none, none], axis=0),
            jnp.concatenate([own_first, none, none, none], axis=0),
            jnp.concatenate([none, none, far_first, far_second], axis=0),
            jnp.concatenate([none, none, far_first, none], axis=0),
        ],
        axis=1,
    ).astype(BF16)


def split(slope):
    high = slope.astype(BF16)
    return high, (slope - high.astype(F32)).astype(BF16)


def force_second(total_ref, own_square_ref, far_square_ref, column_ref, slope_ref, owner):
    for start in range(0, SLOTS, STRIP):
        rows = slice(start, start + STRIP)
        own_high, own_low = split(slope_sixth(own_square_ref[rows, :]))
        slope_ref[rows, 0:256] = own_high
        slope_ref[rows, 256:512] = own_low
        far_high, far_low = split(slope_sixth(far_square_ref[rows, :]))
        slope_ref[rows, 512:768] = far_high
        slope_ref[rows, 768:1024] = far_low
    total_ref[owner, :, 0:32] += lax.dot_general(
        slope_ref[...], column_ref[...], NT, preferred_element_type=F32
    )


def force_scratch():
    square = pltpu.VMEM((SLOTS, SLOTS), F32)
    return [square, square, square, square] + [pltpu.VMEM((32, 4 * SLOTS), BF16)] * 2 + [
        pltpu.VMEM((SLOTS, 4 * SLOTS), BF16)
    ] * 2


def force_self_kernel(own_ref, factor_ref, table_ref, total_ref, *refs):
    total_ref[...] = jnp.zeros_like(total_ref)

    def first_half(cell, buffer):
        factor = factor_ref[pl.ds(cell, 1), :]
        force_first(
            table_ref, refs[buffer], refs[2 + buffer], refs[4 + buffer], cell, own_ref[cell], factor, NO_SHIFT
        )

    def second_half(cell, buffer):
        force_second(total_ref, refs[buffer], refs[2 + buffer], refs[4 + buffer], refs[6 + buffer], cell)

    in_turn(CELLS, first_half, second_half)


def force_cross_kernel(
    which, finish, count_ref, info_ref, shift_ref, table_ref, far_ref, far_factor_ref, *refs
):
    if finish:
        own_ref, factor_ref, before_ref, total_ref, push_ref = refs[:5]
    else:
        before_ref, total_ref = refs[:2]
    list_ref, *refs = refs[-9:]
    amount = listed(which, info_ref, list_ref)

    def first_half(place, buffer):
        owner, _, source, shift = pair_at(list_ref, info_ref, shift_ref, place)
        factor = far_factor_ref[pl.ds(source, 1), :]
        force_first(
            table_ref, refs[buffer], refs[2 + buffer], refs[4 + buffer], owner, far_ref[source], factor, shift
        )

    def second_half(place, buffer):
        _, target, _, _ = pair_at(list_ref, info_ref, shift_ref, place)
        force_second(total_ref, refs[buffer], refs[2 + buffer], refs[4 + buffer], refs[6 + buffer], target)

    in_turn(amount, first_half, second_half)
    if not finish:
        return

    lane = lax.broadcasted_iota(jnp.int32, (1, SLOTS), 1)

    def one_cell(cell):
        sums = total_ref[cell].T
        own = sums[0:8] + sums[8:16]
        far = sums[16:24] + sums[24:32]
        block = own_ref[cell]
        _, place = place_rows(block, NO_SHIFT)
        reach = block[7:8]
        inverse = 1.0 / (reach * reach)
        scale = factor_ref[pl.ds(cell, 1), :] * (6.0 * NORM) * inverse * inverse / reach
        place = place[0:3]
        speed = block[4:7]
        push = scale * (own[0:3] - place * own[3:4]) + (far[0:3] - place * far[3:4])
        warm = jnp.sum(
            speed * place * own[3:4] - speed * own[0:3] - place * own[4:7], axis=0, keepdims=True
        )
        warm = scale * (warm + own[7:8])
        live = lane < count_ref[cell]
        push_ref[cell, 0:3, :] = jnp.where(live, push, 0.0)
        push_ref[cell, 3:4, :] = jnp.where(live, warm, 0.0)

    def some_cells(step, carry):
        for part in range(4):
            one_cell(step * 4 + part)
        return carry

    lax.fori_loop(0, CELLS // 4, some_cells, 0)


def sort_kernel(owner_ref, cell_ref, mass_ref, mass_out, cell_out, parts_ref):
    span = 256
    devices = 128
    device_row = row_index((devices, span))
    before = (row_index((span, span)) <= lax.broadcasted_iota(jnp.int32, (span, span), 1)).astype(BF16)
    parts_ref[...] = jnp.zeros_like(parts_ref)

    def chunk(step, taken):
        owner = owner_ref[pl.ds(step, 1), :]
        cell = cell_ref[pl.ds(step, 1), :]
        mass = mass_ref[pl.ds(step, 1), :]
        chosen = device_row == owner
        ones = chosen.astype(F32)
        upto = lax.dot_general(ones.astype(BF16), before, NN, preferred_element_type=F32)
        rank = jnp.sum(ones * (upto + taken), axis=0, keepdims=True) - 1.0
        slot = (device_row.astype(F32) == rank).astype(F32).astype(BF16)
        mass_parts = thirds(mass)
        cell_parts = (
            (cell & 63).astype(F32),
            ((cell >> 6) & 63).astype(F32),
            (cell >> 12).astype(F32),
        )
        values = [jnp.where(chosen, part, 0.0).astype(BF16) for part in mass_parts + cell_parts]
        parts_ref[...] += lax.dot_general(
            jnp.concatenate(values, axis=0), slot, NT, preferred_element_type=F32
        )
        return taken + upto[:, span - 1 : span]

    lax.fori_loop(0, owner_ref.shape[0], chunk, jnp.zeros((devices, 1), F32))
    n = devices
    mass_out[...] = (parts_ref[0:n] + parts_ref[n : 2 * n]) + parts_ref[2 * n : 3 * n]
    cell_out[...] = (
        parts_ref[3 * n : 4 * n]
        + 64.0 * parts_ref[4 * n : 5 * n]
        + 4096.0 * parts_ref[5 * n : 6 * n]
    )


def put_line(ref, line, rows):
    ref[pl.Slice(line, 128, 16), :] = rows[:, 0:128]
    ref[pl.Slice(8 + line, 128, 16), :] = rows[:, 128:256]


def get_line(ref, line):
    return jnp.concatenate(
        [ref[pl.Slice(line, 128, 16), :], ref[pl.Slice(8 + line, 128, 16), :]], axis=1
    )


def dot32(left, right):
    return lax.dot_general(left, right, NN, precision=highest, preferred_element_type=F32)


def deposit_kernel(mass_ref, cell_ref, z_ref, y_ref, out_ref, grid_ref):
    lanes = 128
    planes = grid_ref.shape[0]
    rows_at = row_index((planes, lanes))
    deep_at = row_index((M, lanes))
    grid_ref[...] = jnp.zeros_like(grid_ref)
    group = 8

    def chunk(step, carry):
        left, first, second = [], [], []
        for part in range(group):
            cell = cell_ref[pl.ds(step * group + part, 1), :].astype(jnp.int32)
            mass = mass_ref[pl.ds(step * group + part, 1), :]
            high = rounded(mass)
            low = mass - high
            left.append((rows_at == (cell >> 8)).astype(F32).astype(BF16))
            named = deep_at == (cell & 255)
            first.append(jnp.where(named, high, 0.0).astype(BF16))
            second.append(jnp.where(named, low, 0.0).astype(BF16))
        left = jnp.concatenate(left + left, axis=1)
        right = jnp.concatenate(first + second, axis=1)
        grid_ref[...] += lax.dot_general(left, right, NT, preferred_element_type=F32)
        return carry

    lax.fori_loop(0, mass_ref.shape[0] // group, chunk, 0)
    for plane in range(planes // M):
        piece = grid_ref[plane * M : (plane + 1) * M, :]
        turned = jnp.concatenate(
            [dot32(piece, z_ref[:, 0:M]), dot32(piece, z_ref[:, M : 2 * M])], axis=0
        )
        for part in range(4):
            rows = dot32(y_ref[part * 128 : (part + 1) * 128, :], turned)
            put_line(out_ref, plane * 4 + part, rows)


def filter_kernel(first_ref, in_ref, forward_ref, back_ref, out_ref):
    for line in range(2):
        pieces = [
            get_line(in_ref, plane * 4 + part * 2 + line)
            for part in range(2)
            for plane in range(2)
        ]
        spectrum = dot32(forward_ref[...], jnp.concatenate(pieces, axis=0))
        along_x = row_index((M, M))
        along_z = lax.broadcasted_iota(jnp.int32, (M, M), 1)
        along_x = jnp.where(along_x < M // 2, along_x, along_x - M)
        along_z = jnp.where(along_z < M // 2, along_z, along_z - M)
        along_y = first_ref[0] + line
        along_y = jnp.where(along_y < M // 2, along_y, along_y - M)
        square = (along_x * along_x + along_z * along_z + along_y * along_y).astype(F32)
        step = 2.0 * math.pi / M
        green = jnp.where(square > 0, -1.0 / (step * step * jnp.maximum(square, 1.0)), 0.0)
        spectrum = jnp.concatenate([spectrum[0:M] * green, spectrum[M : 2 * M] * green], axis=0)
        result = dot32(back_ref[...], spectrum)
        for piece in range(4):
            part, plane = piece // 2, piece % 2
            put_line(
                out_ref, plane * 4 + part * 2 + line, result[piece * 128 : (piece + 1) * 128]
            )


def potential_kernel(in_ref, y_ref, z_ref, out_ref):
    for plane in range(2):
        pieces = [get_line(in_ref, plane * 4 + part) for part in range(4)]
        turned = dot32(y_ref[...], jnp.concatenate(pieces, axis=0))
        out_ref[plane] = dot32(turned[0:M], z_ref[0:M, :]) + dot32(
            turned[M : 2 * M], z_ref[M : 2 * M, :]
        )


def wave_tables():
    index = np.arange(M)
    angle = 2.0 * np.pi / M * (np.outer(index, index) % M)
    cosine, sine = np.cos(angle), np.sin(angle)
    pairs = np.concatenate([index[0::2], index[1::2]])
    z_forward = np.concatenate([cosine, -sine], axis=1)
    y_forward = np.block([[cosine[pairs], sine[pairs]], [-sine[pairs], cosine[pairs]]])
    x_forward = np.block([[cosine[:, pairs], sine[:, pairs]], [-sine[:, pairs], cosine[:, pairs]]])
    x_back = np.block([[cosine[pairs], -sine[pairs]], [sine[pairs], cosine[pairs]]])
    y_back = np.block([[cosine[:, pairs], -sine[:, pairs]], [sine[:, pairs], cosine[:, pairs]]])
    z_back = np.concatenate([cosine, -sine], axis=0) / float(M) ** 3
    return [
        np.asarray(item, np.float32)
        for item in (z_forward, y_forward, x_forward, x_back, y_back, z_back)
    ]


def per_device(
    positions,
    velocities,
    masses,
    smoothing,
    energies,
    cell_counts,
    pair_list,
    export_list,
    mesh_owner,
    mesh_cell,
):
    devices = lax.axis_size("cells")
    me = lax.axis_index("cells").astype(jnp.int32)
    slots_iota = jnp.arange(SLOTS, dtype=jnp.int32)
    live = (slots_iota[None, :] < cell_counts[:, None]).astype(F32)
    heat = energies.reshape(CELLS, SLOTS)
    mass = masses.reshape(CELLS, SLOTS) * live
    own = jnp.concatenate(
        [
            positions.reshape(3, CELLS, SLOTS),
            (mass / SLOTS)[None],
            velocities.reshape(3, CELLS, SLOTS),
            smoothing.reshape(1, CELLS, SLOTS),
        ],
        axis=0,
    ).transpose(1, 0, 2)

    groups_a = [list(range(g, g + GROUP)) for g in range(0, devices, GROUP)]
    groups_b = [[(i + GROUP // 2) % devices for i in g] for g in groups_a]
    exports = export_list[0]
    lane32 = jnp.arange(GROUP, dtype=jnp.int32)

    def wanted(others):
        step = (me - others + devices // 2) % devices - devices // 2
        row = jnp.where(step < 0, step + HALF, step + HALF - 1)
        row = jnp.clip(row, 0, 2 * HALF - 1)
        return jnp.maximum(jnp.take(exports, row, axis=0), 0).reshape(-1)

    to_a = wanted(me // GROUP * GROUP + lane32)
    start_b = (me - GROUP // 2) % devices // GROUP * GROUP + GROUP // 2
    to_b = wanted((start_b + lane32) % devices)

    def swap(data, groups):
        return lax.all_to_all(data, "cells", 0, 0, axis_index_groups=groups, tiled=True)

    far_a = swap(jnp.take(own, to_a, axis=0), groups_a)
    far_b = swap(jnp.take(own, to_b, axis=0), groups_b)

    owner_cell, neighbour, slot, direction = (pair_list[i] for i in range(4))
    step = jnp.where(neighbour < HALF, neighbour - HALF, neighbour - HALF + 1)
    other = (me + step) % devices
    in_a = other // GROUP == me // GROUP
    place = jnp.where(in_a, other % GROUP, (other - GROUP // 2) % GROUP)
    info = jnp.stack([owner_cell, place * CAP + slot, jnp.where(in_a, 0, 1)]).astype(jnp.int32)
    shift = jnp.stack([direction // 9 - 1, direction // 3 % 3 - 1, direction % 3 - 1]).astype(F32)

    lines = CELLS * SLOTS // 256
    mass_sent, cell_sent = pl.pallas_call(
        sort_kernel,
        out_shape=[jax.ShapeDtypeStruct((devices, 128), F32)] * 2,
        in_specs=[VMEM] * 3,
        out_specs=[VMEM] * 2,
        scratch_shapes=[pltpu.VMEM((6 * 128, 128), F32)],
        compiler_params=params(32),
        cost_estimate=cost(6e9, 1e6),
        name="sort_masses",
    )(mesh_owner.reshape(lines, 256), mesh_cell.reshape(lines, 256), mass.reshape(lines, 256))

    table, total = pl.pallas_call(
        density_self_kernel,
        out_shape=[
            jax.ShapeDtypeStruct((CELLS, SLOTS, 128), BF16),
            jax.ShapeDtypeStruct((CELLS + 1, SLOTS, 128), F32),
        ],
        in_specs=[VMEM],
        out_specs=[VMEM] * 2,
        scratch_shapes=[pltpu.VMEM((SLOTS, SLOTS), F32)] * 2,
        compiler_params=params(32),
        cost_estimate=cost(8e9, 1e6),
        name="density_self",
    )(own)

    def density_cross(which, far, total, finish):
        out_shape = [jax.ShapeDtypeStruct((CELLS + 1, SLOTS, 128), F32)]
        extra = (total,)
        if finish:
            out_shape += [jax.ShapeDtypeStruct((CELLS, SLOTS), F32)] * 2
            extra = (own, heat, total)
        return pl.pallas_call(
            functools.partial(density_cross_kernel, which, finish),
            out_shape=out_shape,
            in_specs=[SMEM] * 3 + [VMEM] * (2 + len(extra)),
            out_specs=[VMEM] * len(out_shape),
            input_output_aliases={4 + len(extra): 0},
            scratch_shapes=[pltpu.SMEM((256,), jnp.int32)] + [pltpu.VMEM((SLOTS, SLOTS), F32)] * 2,
            compiler_params=params(40),
            cost_estimate=cost(1e10, 1e6),
            name="density_cross",
        )(cell_counts, info, shift, table, far, *extra)

    (total,) = density_cross(0, far_a, total, False)
    _, density, factor = density_cross(1, far_b, total, True)

    factor_a = swap(jnp.take(factor, to_a, axis=0), groups_a)
    factor_b = swap(jnp.take(factor, to_b, axis=0), groups_b)

    total = pl.pallas_call(
        force_self_kernel,
        out_shape=jax.ShapeDtypeStruct((CELLS + 1, SLOTS, 128), F32),
        in_specs=[VMEM] * 3,
        out_specs=VMEM,
        scratch_shapes=force_scratch(),
        compiler_params=params(40),
        cost_estimate=cost(1.5e10, 1e6),
        name="force_self",
    )(own, factor, table)

    def force_cross(which, far, far_factor, total, finish):
        out_shape = [jax.ShapeDtypeStruct((CELLS + 1, SLOTS, 128), F32)]
        extra = (total,)
        if finish:
            out_shape += [jax.ShapeDtypeStruct((CELLS, 4, SLOTS), F32)]
            extra = (own, factor, total)
        return pl.pallas_call(
            functools.partial(force_cross_kernel, which, finish),
            out_shape=out_shape,
            in_specs=[SMEM] * 3 + [VMEM] * (3 + len(extra)),
            out_specs=[VMEM] * len(out_shape),
            input_output_aliases={5 + len(extra): 0},
            scratch_shapes=[pltpu.SMEM((256,), jnp.int32)] + force_scratch(),
            compiler_params=params(40),
            cost_estimate=cost(3e10, 1e6),
            name="force_cross",
        )(cell_counts, info, shift, table, far, far_factor, *extra)

    (total,) = force_cross(0, far_a, factor_a, total, False)
    _, push = force_cross(1, far_b, factor_b, total, True)
    acceleration = push[:, 0:3].transpose(1, 0, 2).reshape(3, -1)
    heating = push[:, 3].reshape(-1)

    z_forward, y_forward, x_forward, x_back, y_back, z_back = wave_tables()
    swapped = swap(jnp.stack([mass_sent, cell_sent], axis=1), None)
    wide = jax.ShapeDtypeStruct((devices * 16, M // 2), F32)
    half_way = pl.pallas_call(
        deposit_kernel,
        out_shape=wide,
        in_specs=[VMEM] * 4,
        out_specs=VMEM,
        scratch_shapes=[pltpu.VMEM((2 * M, M), F32)],
        compiler_params=params(48),
        cost_estimate=cost(1.5e10, 1e6),
        name="deposit",
    )(swapped[:, 0], swapped[:, 1], z_forward, y_forward)
    half_way = swap(half_way.reshape(devices, 16, M // 2), None)
    back = pl.pallas_call(
        filter_kernel,
        out_shape=wide,
        in_specs=[SMEM] + [VMEM] * 3,
        out_specs=VMEM,
        compiler_params=params(48),
        cost_estimate=cost(5e9, 1e6),
        name="filter",
    )((2 * me).reshape(1), half_way.reshape(devices * 16, M // 2), x_forward, x_back)
    back = swap(back.reshape(devices, 16, M // 2), None)
    potential = pl.pallas_call(
        potential_kernel,
        out_shape=jax.ShapeDtypeStruct((2, M, M), F32),
        in_specs=[VMEM] * 3,
        out_specs=VMEM,
        compiler_params=params(48),
        cost_estimate=cost(4e9, 1e6),
        name="potential",
    )(back.reshape(devices * 16, M // 2), y_back, z_back)
    return (density.reshape(-1), acceleration, heating, potential)


def solution(mesh):
    in_specs = (
        P(None, "cells"),
        P(None, "cells"),
        P("cells"),
        P("cells"),
        P("cells"),
        P("cells"),
        P(None, "cells"),
        P("cells", None, None),
        P("cells", None),
        P("cells"),
    )
    out_specs = (P("cells"), P(None, "cells"), P("cells"), P("cells", None, None))
    return jax.shard_map(
        per_device, mesh=mesh, in_specs=in_specs, out_specs=out_specs, check_vma=False
    )
```

```python
import functools
import math

import jax
import jax.numpy as jnp
import numpy as np
from jax import lax
from jax.experimental import pallas as pl
from jax.experimental.pallas import tpu as pltpu
from jax.sharding import PartitionSpec as P

M = 256
GROUP = 32
CAP = 8
HALF = 13
CELLS = 32
SLOTS = 256
STRIP = 32
TOGETHER = 8
F32 = jnp.float32
BF16 = jnp.bfloat16
NORM = 8.0 / math.pi
TINY = 1e-30
VMEM = pl.BlockSpec(memory_space=pltpu.VMEM)
SMEM = pl.BlockSpec(memory_space=pltpu.SMEM)
NT = (((1,), (1,)), ((), ()))
NN = (((1,), (0,)), ((), ()))
TN = (((0,), (0,)), ((), ()))
NO_SHIFT = (0.0, 0.0, 0.0)
highest = lax.Precision.HIGHEST


def params(mib):
    return pltpu.CompilerParams(vmem_limit_bytes=mib * 1024 * 1024)


def cost(flops, nbytes):
    return pl.CostEstimate(
        flops=int(flops / 6), bytes_accessed=int(nbytes / 10), transcendentals=0
    )


def row_index(shape):
    return lax.broadcasted_iota(jnp.int32, shape, 0)


def rounded(value):
    return value.astype(BF16).astype(F32)


def thirds(value):
    first = rounded(value)
    rest = value - first
    second = rounded(rest)
    return first, second, rest - second


def place_rows(block, shift):
    row = row_index(block.shape)
    moved = jnp.where(row == 0, shift[0], jnp.where(row == 1, shift[1], shift[2])) - 0.5
    return row, jnp.where(row < 3, block + moved, 0.0)


def far_stack(basis):
    first, second, third = thirds(basis)
    return jnp.concatenate([first, second, first, second, third, first], axis=0)


def own_stack(basis):
    first, second, third = thirds(basis)
    return jnp.concatenate([first, first, second, second, first, third], axis=0)


def far_basis(block, shift):
    row, place = place_rows(block, shift)
    square = jnp.sum(place * place, axis=0, keepdims=True)
    basis = jnp.where(row == 3, square, jnp.where(row == 4, 1.0, place))
    return row, place, basis


def own_tables(own_ref, scaled_ref, table_ref):
    zeros = jnp.zeros((80, SLOTS), F32)

    def some_cells(step, carry):
        for part in range(4):
            cell = step * 4 + part
            row, place = place_rows(own_ref[cell], NO_SHIFT)
            square = jnp.sum(place * place, axis=0, keepdims=True)
            basis = jnp.where(
                row < 3, -2.0 * place, jnp.where(row == 3, 1.0, jnp.where(row == 4, square, 0.0))
            )
            table_ref[cell] = own_stack(basis).astype(BF16)
            scaled = own_stack(basis * own_inverse(own_ref, cell))
            scaled_ref[cell] = jnp.concatenate([scaled, zeros], axis=0).T.astype(BF16)
        return carry

    lax.fori_loop(0, CELLS // 4, some_cells, 0)


def kernel_half(square):
    square = jnp.maximum(square, TINY)
    dist = square * lax.rsqrt(square)
    left = jnp.maximum(1.0 - dist, 0.0)
    inner = 0.5 - 3.0 * square * left
    outer = left * left * left
    return jnp.where(square <= 0.25, inner, outer)


def slope_sixth(square):
    square = jnp.minimum(square, 1.0)
    inverse = lax.rsqrt(square)
    dist = square * inverse
    inner = 3.0 * dist - 2.0
    outer = (2.0 - dist) - inverse
    return jnp.where(square <= 0.25, inner, outer)


def together(amount, first_half, second_half):
    def some_pairs(step, carry):
        for part in range(TOGETHER):
            first_half(step * TOGETHER + part, part)
        for part in range(TOGETHER):
            second_half(step * TOGETHER + part, part)
        return carry

    lax.fori_loop(0, amount // TOGETHER, some_pairs, 0)


def density_pairs(amount, scaled_ref, total_ref, square_refs, pair):
    def first_half(place, part):
        owner, _, block, shift = pair(place)
        _, _, basis = far_basis(block, shift)
        square_refs[part][...] = lax.dot_general(
            scaled_ref[owner, :, 0:48],
            far_stack(basis).astype(BF16),
            NN,
            preferred_element_type=F32,
        )

    def second_half(place, part):
        _, target, block, _ = pair(place)
        weight = block[3:4]
        for start in range(0, SLOTS, STRIP):
            rows = slice(start, start + STRIP)
            terms = kernel_half(square_refs[part][rows, :]) * weight
            total_ref[target, rows, :] += terms[:, 0:128] + terms[:, 128:256]

    together(amount, first_half, second_half)


def own_inverse(own_ref, owner):
    reach = own_ref[owner, 7:8, :]
    return 1.0 / (reach * reach)


def listed(which, info_ref, list_ref):
    pairs = info_ref.shape[1]

    def one_pair(pair, found):
        list_ref[found] = pair
        return found + (info_ref[2, pair] == which).astype(jnp.int32)

    found = lax.fori_loop(0, pairs, one_pair, jnp.int32(0))
    for spare in range(TOGETHER - 1):
        list_ref[found + spare] = pairs
    return (found + TOGETHER - 1) // TOGETHER * TOGETHER


def pair_at(list_ref, info_ref, shift_ref, place):
    pair = list_ref[place]
    real = pair < info_ref.shape[1]
    pair = jnp.minimum(pair, info_ref.shape[1] - 1)
    owner = info_ref[0, pair]
    shift = (shift_ref[0, pair], shift_ref[1, pair], shift_ref[2, pair])
    return owner, jnp.where(real, owner, CELLS), info_ref[1, pair], shift


def density_scratch():
    return [pltpu.VMEM((SLOTS, SLOTS), F32)] * TOGETHER


def summed(total_ref, cell):
    return jnp.sum(total_ref[cell].T, axis=0, keepdims=True)


def density_self_kernel(own_ref, scaled_ref, table_ref, sum_ref, total_ref, *square_refs):
    own_tables(own_ref, scaled_ref, table_ref)
    total_ref[...] = jnp.zeros_like(total_ref)
    density_pairs(
        CELLS,
        scaled_ref,
        total_ref,
        square_refs,
        lambda cell: (cell, cell, own_ref[cell], NO_SHIFT),
    )

    def some_cells(step, carry):
        for part in range(4):
            cell = step * 4 + part
            sum_ref[pl.ds(cell, 1), :] = summed(total_ref, cell)
        return carry

    lax.fori_loop(0, CELLS // 4, some_cells, 0)


def density_cross_kernel(
    which, finish, count_ref, info_ref, shift_ref, scaled_ref, own_ref, far_ref, *refs
):
    if finish:
        heat_ref, before_ref, density_ref, factor_ref = refs[:4]
    else:
        before_ref, sum_ref = refs[:2]
    total_ref, list_ref, *square_refs = refs[-2 - TOGETHER :]
    amount = listed(which, info_ref, list_ref)
    total_ref[...] = jnp.zeros_like(total_ref)

    def pair(place):
        owner, target, source, shift = pair_at(list_ref, info_ref, shift_ref, place)
        return owner, target, far_ref[source], shift

    density_pairs(amount, scaled_ref, total_ref, square_refs, pair)
    lane = lax.broadcasted_iota(jnp.int32, (1, SLOTS), 1)

    def some_cells(step, carry):
        for part in range(4):
            cell = step * 4 + part
            line = pl.ds(cell, 1)
            raw = summed(total_ref, cell) + before_ref[line, :]
            if not finish:
                sum_ref[line, :] = raw
                continue
            reach = own_ref[cell, 7:8, :]
            raw = raw * (2.0 * NORM) / (reach * reach * reach)
            density = jnp.where(lane < count_ref[cell], raw, 1.0)
            density_ref[line, :] = density
            factor_ref[line, :] = 2.0 / 3.0 * heat_ref[line, :] / density
        return carry

    lax.fori_loop(0, CELLS // 4, some_cells, 0)


def force_first(table_ref, square_ref, column_ref, line_ref, owner, block, factor, shift):
    row, place, basis = far_basis(block, shift)
    square_ref[...] = lax.dot_general(
        far_stack(basis).astype(BF16), table_ref[owner], TN, preferred_element_type=F32
    )
    reach = block[7:8]
    weight = block[3:4]
    inverse = 1.0 / (reach * reach)
    column_ref[...] = jnp.broadcast_to(jnp.broadcast_to(inverse, (8, SLOTS)).T[:, 0:1], (SLOTS, 128))
    swirl = jnp.sum(place[0:3] * block[4:7], axis=0, keepdims=True)
    own_side = jnp.where(
        row < 3, place, jnp.where(row == 3, 1.0, jnp.where(row == 7, swirl, block))
    )
    own_side = own_side * weight
    far_side = jnp.where(row < 3, place, jnp.where(row == 3, 1.0, 0.0))
    far_side = far_side * (weight * factor * (6.0 * NORM) * inverse * inverse / reach)
    own_first = rounded(own_side)
    own_second = own_side - own_first
    far_first = rounded(far_side)
    far_second = far_side - far_first
    none = jnp.zeros((8, SLOTS), F32)
    line_ref[...] = jnp.concatenate(
        [
            jnp.concatenate([own_first, own_second, none, none], axis=0),
            jnp.concatenate([own_first, none, none, none], axis=0),
            jnp.concatenate([none, none, far_first, far_second], axis=0),
            jnp.concatenate([none, none, far_first, none], axis=0),
        ],
        axis=1,
    ).astype(BF16)


def split(slope):
    high = slope.astype(BF16)
    return high, (slope - high.astype(F32)).astype(BF16)


def force_second(total_ref, square_ref, column_ref, line_ref, slope_ref, target, inverse):
    for start in range(0, SLOTS, STRIP):
        rows = slice(start, start + STRIP)
        square = jnp.maximum(square_ref[rows, :], TINY)
        far_inverse = column_ref[rows, :]
        far_inverse = jnp.concatenate([far_inverse, far_inverse], axis=1)
        own_high, own_low = split(slope_sixth(square * inverse))
        far_high, far_low = split(slope_sixth(square * far_inverse))
        for part, piece in enumerate((own_high, own_low, far_high, far_low)):
            slope_ref[part * SLOTS + start : part * SLOTS + start + STRIP, :] = piece
    total_ref[target] += lax.dot_general(
        line_ref[...], slope_ref[...], NN, preferred_element_type=F32
    )


def force_scratch():
    return (
        [pltpu.VMEM((SLOTS, SLOTS), F32)] * TOGETHER
        + [pltpu.VMEM((SLOTS, 128), F32)] * TOGETHER
        + [pltpu.VMEM((32, 4 * SLOTS), BF16)] * TOGETHER
        + [pltpu.VMEM((4 * SLOTS, SLOTS), BF16)] * TOGETHER
    )


def force_pairs(amount, table_ref, own_ref, total_ref, refs, pair):
    def first_half(place, part):
        owner, _, block, factor, shift = pair(place)
        force_first(
            table_ref, *refs[part : 3 * TOGETHER : TOGETHER], owner, block, factor, shift
        )

    def second_half(place, part):
        owner, target, _, _, _ = pair(place)
        force_second(total_ref, *refs[part::TOGETHER], target, own_inverse(own_ref, owner))

    together(amount, first_half, second_half)


def force_self_kernel(own_ref, factor_ref, table_ref, total_ref, *refs):
    total_ref[...] = jnp.zeros_like(total_ref)

    def pair(cell):
        return cell, cell, own_ref[cell], factor_ref[pl.ds(cell, 1), :], NO_SHIFT

    force_pairs(CELLS, table_ref, own_ref, total_ref, refs, pair)


def force_cross_kernel(
    count_ref,
    info_ref,
    shift_ref,
    table_ref,
    own_ref,
    far_a_ref,
    far_b_ref,
    far_factor_ref,
    factor_ref,
    before_ref,
    push_ref,
    total_ref,
    list_ref,
    *refs,
):
    total_ref[...] = before_ref[...]
    for which, far_ref in enumerate((far_a_ref, far_b_ref)):
        amount = listed(which, info_ref, list_ref)

        def pair(place, far_ref=far_ref):
            owner, target, source, shift = pair_at(list_ref, info_ref, shift_ref, place)
            line = info_ref[3, jnp.minimum(list_ref[place], info_ref.shape[1] - 1)]
            return owner, target, far_ref[source], far_factor_ref[pl.ds(line, 1), :], shift

        force_pairs(amount, table_ref, own_ref, total_ref, refs, pair)

    lane = lax.broadcasted_iota(jnp.int32, (1, SLOTS), 1)

    def some_cells(step, carry):
        for part in range(4):
            cell = step * 4 + part
            sums = total_ref[cell]
            own = sums[0:8] + sums[8:16]
            far = sums[16:24] + sums[24:32]
            block = own_ref[cell]
            _, place = place_rows(block, NO_SHIFT)
            reach = block[7:8]
            inverse = 1.0 / (reach * reach)
            scale = factor_ref[pl.ds(cell, 1), :] * (6.0 * NORM) * inverse * inverse / reach
            place = place[0:3]
            speed = block[4:7]
            push = scale * (own[0:3] - place * own[3:4]) + (far[0:3] - place * far[3:4])
            warm = jnp.sum(
                speed * place * own[3:4] - speed * own[0:3] - place * own[4:7],
                axis=0,
                keepdims=True,
            )
            warm = scale * (warm + own[7:8])
            live = lane < count_ref[cell]
            push = jnp.where(live, push, 0.0)
            for line in range(3):
                push_ref[line, pl.ds(cell, 1), :] = push[line : line + 1]
            push_ref[3, pl.ds(cell, 1), :] = jnp.where(live, warm, 0.0)
        return carry

    lax.fori_loop(0, CELLS // 4, some_cells, 0)


def sort_kernel(owner_ref, cell_ref, mass_ref, mass_out, cell_out, parts_ref):
    span = 256
    together = 4
    devices = 128
    device_row = row_index((devices, span))
    slot_row = device_row.astype(F32)
    before = (
        row_index((span, span)) <= lax.broadcasted_iota(jnp.int32, (span, span), 1)
    ).astype(F32).astype(BF16)
    parts_ref[...] = jnp.zeros_like(parts_ref)

    def chunk(step, taken):
        named, values = [], []
        for part in range(together):
            line = pl.ds(step * together + part, 1)
            cell = cell_ref[line, :]
            chosen = device_row == owner_ref[line, :]
            ones = chosen.astype(F32)
            upto = lax.dot_general(ones.astype(BF16), before, NN, preferred_element_type=F32)
            rank = jnp.sum(ones * (upto + taken), axis=0, keepdims=True) - 1.0
            taken = taken + upto[:, span - 1 : span]
            named.append((slot_row == rank).astype(F32).astype(BF16))
            parts = thirds(mass_ref[line, :]) + (
                (cell & 63).astype(F32),
                ((cell >> 6) & 63).astype(F32),
                (cell >> 12).astype(F32),
            )
            values.append(
                jnp.concatenate([jnp.where(chosen, item, 0.0) for item in parts], axis=0).astype(BF16)
            )
        parts_ref[...] += lax.dot_general(
            jnp.concatenate(values, axis=1),
            jnp.concatenate(named, axis=1),
            NT,
            preferred_element_type=F32,
        )
        return taken

    lax.fori_loop(0, owner_ref.shape[0] // together, chunk, jnp.zeros((devices, 1), F32))
    n = devices
    mass_out[...] = (parts_ref[0:n] + parts_ref[n : 2 * n]) + parts_ref[2 * n : 3 * n]
    cell_out[...] = (
        parts_ref[3 * n : 4 * n]
        + 64.0 * parts_ref[4 * n : 5 * n]
        + 4096.0 * parts_ref[5 * n : 6 * n]
    )


def put_line(ref, line, rows):
    ref[pl.Slice(line, 128, 16), :] = rows[:, 0:128]
    ref[pl.Slice(8 + line, 128, 16), :] = rows[:, 128:256]


def get_line(ref, line):
    return jnp.concatenate(
        [ref[pl.Slice(line, 128, 16), :], ref[pl.Slice(8 + line, 128, 16), :]], axis=1
    )


def dot32(left, right):
    return lax.dot_general(left, right, NN, precision=highest, preferred_element_type=F32)


def deposit_kernel(mass_ref, cell_ref, z_ref, y_ref, out_ref, grid_ref):
    lanes = 128
    planes = grid_ref.shape[0]
    rows_at = row_index((planes, lanes))
    deep_at = row_index((M, lanes))
    grid_ref[...] = jnp.zeros_like(grid_ref)
    group = 8

    def chunk(step, carry):
        left, first, second = [], [], []
        for part in range(group):
            cell = cell_ref[pl.ds(step * group + part, 1), :].astype(jnp.int32)
            mass = mass_ref[pl.ds(step * group + part, 1), :]
            high = rounded(mass)
            low = mass - high
            left.append((rows_at == (cell >> 8)).astype(F32).astype(BF16))
            named = deep_at == (cell & 255)
            first.append(jnp.where(named, high, 0.0).astype(BF16))
            second.append(jnp.where(named, low, 0.0).astype(BF16))
        left = jnp.concatenate(left + left, axis=1)
        right = jnp.concatenate(first + second, axis=1)
        grid_ref[...] += lax.dot_general(left, right, NT, preferred_element_type=F32)
        return carry

    lax.fori_loop(0, mass_ref.shape[0] // group, chunk, 0)
    for plane in range(planes // M):
        piece = grid_ref[plane * M : (plane + 1) * M, :]
        turned = jnp.concatenate(
            [dot32(piece, z_ref[:, 0:M]), dot32(piece, z_ref[:, M : 2 * M])], axis=0
        )
        for part in range(4):
            rows = dot32(y_ref[part * 128 : (part + 1) * 128, :], turned)
            put_line(out_ref, plane * 4 + part, rows)


def filter_kernel(first_ref, in_ref, forward_ref, back_ref, out_ref):
    for line in range(2):
        pieces = [
            get_line(in_ref, plane * 4 + part * 2 + line)
            for part in range(2)
            for plane in range(2)
        ]
        spectrum = dot32(forward_ref[...], jnp.concatenate(pieces, axis=0))
        along_x = row_index((M, M))
        along_z = lax.broadcasted_iota(jnp.int32, (M, M), 1)
        along_x = jnp.where(along_x < M // 2, along_x, along_x - M)
        along_z = jnp.where(along_z < M // 2, along_z, along_z - M)
        along_y = first_ref[0] + line
        along_y = jnp.where(along_y < M // 2, along_y, along_y - M)
        square = (along_x * along_x + along_z * along_z + along_y * along_y).astype(F32)
        step = 2.0 * math.pi / M
        green = jnp.where(square > 0, -1.0 / (step * step * jnp.maximum(square, 1.0)), 0.0)
        spectrum = jnp.concatenate([spectrum[0:M] * green, spectrum[M : 2 * M] * green], axis=0)
        result = dot32(back_ref[...], spectrum)
        for piece in range(4):
            part, plane = piece // 2, piece % 2
            put_line(
                out_ref, plane * 4 + part * 2 + line, result[piece * 128 : (piece + 1) * 128]
            )


def potential_kernel(in_ref, y_ref, z_ref, out_ref):
    for plane in range(2):
        pieces = [get_line(in_ref, plane * 4 + part) for part in range(4)]
        turned = dot32(y_ref[...], jnp.concatenate(pieces, axis=0))
        out_ref[plane] = dot32(turned[0:M], z_ref[0:M, :]) + dot32(
            turned[M : 2 * M], z_ref[M : 2 * M, :]
        )


def wave_tables():
    index = np.arange(M)
    angle = 2.0 * np.pi / M * (np.outer(index, index) % M)
    cosine, sine = np.cos(angle), np.sin(angle)
    pairs = np.concatenate([index[0::2], index[1::2]])
    z_forward = np.concatenate([cosine, -sine], axis=1)
    y_forward = np.block([[cosine[pairs], sine[pairs]], [-sine[pairs], cosine[pairs]]])
    x_forward = np.block([[cosine[:, pairs], sine[:, pairs]], [-sine[:, pairs], cosine[:, pairs]]])
    x_back = np.block([[cosine[pairs], -sine[pairs]], [sine[pairs], cosine[pairs]]])
    y_back = np.block([[cosine[:, pairs], -sine[:, pairs]], [sine[:, pairs], cosine[:, pairs]]])
    z_back = np.concatenate([cosine, -sine], axis=0) / float(M) ** 3
    return [
        np.asarray(item, np.float32)
        for item in (z_forward, y_forward, x_forward, x_back, y_back, z_back)
    ]


def per_device(
    positions,
    velocities,
    masses,
    smoothing,
    energies,
    cell_counts,
    pair_list,
    export_list,
    mesh_owner,
    mesh_cell,
):
    devices = lax.axis_size("cells")
    me = lax.axis_index("cells").astype(jnp.int32)
    slots_iota = jnp.arange(SLOTS, dtype=jnp.int32)
    live = (slots_iota[None, :] < cell_counts[:, None]).astype(F32)
    heat = energies.reshape(CELLS, SLOTS)
    mass = masses.reshape(CELLS, SLOTS) * live
    own = jnp.concatenate(
        [
            positions.reshape(3, CELLS, SLOTS),
            (mass / SLOTS)[None],
            velocities.reshape(3, CELLS, SLOTS),
            smoothing.reshape(1, CELLS, SLOTS),
        ],
        axis=0,
    ).transpose(1, 0, 2)

    groups_a = [list(range(g, g + GROUP)) for g in range(0, devices, GROUP)]
    groups_b = [[(i + GROUP // 2) % devices for i in g] for g in groups_a]
    exports = export_list[0]
    lane32 = jnp.arange(GROUP, dtype=jnp.int32)

    def wanted(others):
        step = (me - others + devices // 2) % devices - devices // 2
        row = jnp.where(step < 0, step + HALF, step + HALF - 1)
        row = jnp.clip(row, 0, 2 * HALF - 1)
        return jnp.maximum(jnp.take(exports, row, axis=0), 0).reshape(-1)

    to_a = wanted(me // GROUP * GROUP + lane32)
    start_b = (me - GROUP // 2) % devices // GROUP * GROUP + GROUP // 2
    to_b = wanted((start_b + lane32) % devices)

    def swap(data, groups):
        return lax.all_to_all(data, "cells", 0, 0, axis_index_groups=groups, tiled=True)

    def pick(data, cells):
        return jnp.take(data, cells, axis=0, mode="clip")

    def after(data, *others):
        return lax.optimization_barrier((data, *others))[0]

    sent_a = pick(own, to_a)
    sent_b = pick(own, to_b)
    far_a = swap(sent_a, groups_a)
    mesh_owner, mesh_cell, mass = lax.optimization_barrier((mesh_owner, mesh_cell, mass, sent_a))[:3]

    owner_cell, neighbour, slot, direction = (pair_list[i] for i in range(4))
    step = jnp.where(neighbour < HALF, neighbour - HALF, neighbour - HALF + 1)
    other = (me + step) % devices
    in_a = other // GROUP == me // GROUP
    place = jnp.where(in_a, other % GROUP, (other - GROUP // 2) % GROUP)
    info = jnp.stack(
        [owner_cell, place * CAP + slot, jnp.where(in_a, 0, 1), other * CAP + slot]
    ).astype(jnp.int32)
    shift = jnp.stack([direction // 9 - 1, direction // 3 % 3 - 1, direction % 3 - 1]).astype(F32)

    lines = CELLS * SLOTS // 256
    mass_sent, cell_sent = pl.pallas_call(
        sort_kernel,
        out_shape=[jax.ShapeDtypeStruct((devices, 128), F32)] * 2,
        in_specs=[VMEM] * 3,
        out_specs=[VMEM] * 2,
        scratch_shapes=[pltpu.VMEM((6 * 128, 128), F32)],
        compiler_params=params(32),
        cost_estimate=cost(6e9, 1e6),
        name="sort_masses",
    )(mesh_owner.reshape(lines, 256), mesh_cell.reshape(lines, 256), mass.reshape(lines, 256))

    many = jax.ShapeDtypeStruct((CELLS + 1, 32, SLOTS), F32)
    each = jax.ShapeDtypeStruct((CELLS, SLOTS), F32)
    wide_total = [pltpu.VMEM((CELLS + 1, SLOTS, 128), F32)]
    places = [pltpu.SMEM((256,), jnp.int32)]
    scaled, table, partial = pl.pallas_call(
        density_self_kernel,
        out_shape=[
            jax.ShapeDtypeStruct((CELLS, SLOTS, 128), BF16),
            jax.ShapeDtypeStruct((CELLS, 48, SLOTS), BF16),
            each,
        ],
        in_specs=[VMEM],
        out_specs=[VMEM] * 3,
        scratch_shapes=wide_total + density_scratch(),
        compiler_params=params(40),
        cost_estimate=cost(8e9, 1e6),
        name="density_self",
    )(own)

    swapped = swap(after(jnp.stack([mass_sent, cell_sent], axis=1), far_a, partial), None)
    far_b = swap(after(sent_b, swapped), groups_b)

    def density_cross(which, far, partial, finish):
        extra = (heat, partial) if finish else (partial,)
        out_shape = [each, each] if finish else [each]
        return pl.pallas_call(
            functools.partial(density_cross_kernel, which, finish),
            out_shape=out_shape,
            in_specs=[SMEM] * 3 + [VMEM] * (3 + len(extra)),
            out_specs=[VMEM] * len(out_shape),
            scratch_shapes=wide_total + places + density_scratch(),
            compiler_params=params(40),
            cost_estimate=cost(1e10, 1e6),
            name="density_cross",
        )(cell_counts, info, shift, scaled, own, far, *extra)

    (partial_a,) = density_cross(0, far_a, partial, False)
    density, factor = density_cross(1, far_b, partial_a, True)

    z_forward, y_forward, x_forward, x_back, y_back, z_back = wave_tables()
    wide = jax.ShapeDtypeStruct((devices * 16, M // 2), F32)
    half_way = pl.pallas_call(
        deposit_kernel,
        out_shape=wide,
        in_specs=[VMEM] * 4,
        out_specs=VMEM,
        scratch_shapes=[pltpu.VMEM((2 * M, M), F32)],
        compiler_params=params(48),
        cost_estimate=cost(1.5e10, 1e6),
        name="deposit",
    )(swapped[:, 0], swapped[:, 1], z_forward, y_forward)
    half_way = swap(after(half_way.reshape(devices, 16, M // 2), far_b, partial_a), None)
    to_all = wanted(jnp.arange(devices, dtype=jnp.int32))
    far_factor = swap(after(pick(factor, to_all), half_way), None)

    total = pl.pallas_call(
        force_self_kernel,
        out_shape=many,
        in_specs=[VMEM] * 3,
        out_specs=VMEM,
        scratch_shapes=force_scratch(),
        compiler_params=params(40),
        cost_estimate=cost(1.5e10, 1e6),
        name="force_self",
    )(own, factor, table)

    push = pl.pallas_call(
        force_cross_kernel,
        out_shape=jax.ShapeDtypeStruct((4, CELLS, SLOTS), F32),
        in_specs=[SMEM] * 3 + [VMEM] * 7,
        out_specs=VMEM,
        scratch_shapes=[pltpu.VMEM(many.shape, F32)] + places + force_scratch(),
        compiler_params=params(48),
        cost_estimate=cost(6e10, 1e6),
        name="force_cross",
    )(cell_counts, info, shift, table, own, far_a, far_b, far_factor, factor, total)
    acceleration = push[0:3].reshape(3, -1)
    heating = push[3].reshape(-1)

    back = pl.pallas_call(
        filter_kernel,
        out_shape=wide,
        in_specs=[SMEM] + [VMEM] * 3,
        out_specs=VMEM,
        compiler_params=params(48),
        cost_estimate=cost(5e9, 1e6),
        name="filter",
    )((2 * me).reshape(1), half_way.reshape(devices * 16, M // 2), x_forward, x_back)
    back = swap(after(back.reshape(devices, 16, M // 2), far_factor), None)
    potential = pl.pallas_call(
        potential_kernel,
        out_shape=jax.ShapeDtypeStruct((2, M, M), F32),
        in_specs=[VMEM] * 3,
        out_specs=VMEM,
        compiler_params=params(48),
        cost_estimate=cost(4e9, 1e6),
        name="potential",
    )(back.reshape(devices * 16, M // 2), y_back, z_back)
    return (density.reshape(-1), acceleration, heating, potential)


def solution(mesh):
    in_specs = (
        P(None, "cells"),
        P(None, "cells"),
        P("cells"),
        P("cells"),
        P("cells"),
        P("cells"),
        P(None, "cells"),
        P("cells", None, None),
        P("cells", None),
        P("cells"),
    )
    out_specs = (P("cells"), P(None, "cells"), P("cells"), P("cells", None, None))
    return jax.shard_map(
        per_device, mesh=mesh, in_specs=in_specs, out_specs=out_specs, check_vma=False
    )
```

```python
import functools
import math

import jax
import jax.numpy as jnp
import numpy as np
from jax import lax
from jax.experimental import pallas as pl
from jax.experimental.pallas import tpu as pltpu
from jax.sharding import PartitionSpec as P

M = 256
GROUP = 32
CAP = 8
HALF = 13
CELLS = 32
SLOTS = 256
STRIP = 32
TOGETHER = 8
EARLY = 64
F32 = jnp.float32
BF16 = jnp.bfloat16
NORM = 8.0 / math.pi
TINY = 1e-30
VMEM = pl.BlockSpec(memory_space=pltpu.VMEM)
SMEM = pl.BlockSpec(memory_space=pltpu.SMEM)
NT = (((1,), (1,)), ((), ()))
NN = (((1,), (0,)), ((), ()))
TN = (((0,), (0,)), ((), ()))
NO_SHIFT = (0.0, 0.0, 0.0)
highest = lax.Precision.HIGHEST


def params(mib):
    return pltpu.CompilerParams(vmem_limit_bytes=mib * 1024 * 1024)


def cost(flops, nbytes):
    return pl.CostEstimate(
        flops=int(flops / 6), bytes_accessed=int(nbytes / 10), transcendentals=0
    )


def row_index(shape):
    return lax.broadcasted_iota(jnp.int32, shape, 0)


def rounded(value):
    return value.astype(BF16).astype(F32)


def thirds(value):
    first = rounded(value)
    rest = value - first
    second = rounded(rest)
    return first, second, rest - second


def place_rows(block, shift):
    row = row_index(block.shape)
    moved = jnp.where(row == 0, shift[0], jnp.where(row == 1, shift[1], shift[2])) - 0.5
    return row, jnp.where(row < 3, block + moved, 0.0)


def far_stack(basis):
    first, second, third = thirds(basis)
    return jnp.concatenate([first, second, first, second, third, first], axis=0)


def own_stack(basis):
    first, second, third = thirds(basis)
    return jnp.concatenate([first, first, second, second, first, third], axis=0)


def far_basis(block, shift):
    row, place = place_rows(block, shift)
    square = jnp.sum(place * place, axis=0, keepdims=True)
    basis = jnp.where(row == 3, square, jnp.where(row == 4, 1.0, place))
    return row, place, basis


def own_tables(own_ref, scaled_ref, table_ref):
    def some_cells(step, carry):
        for part in range(4):
            cell = step * 4 + part
            row, place = place_rows(own_ref[cell], NO_SHIFT)
            square = jnp.sum(place * place, axis=0, keepdims=True)
            basis = jnp.where(
                row < 3, -2.0 * place, jnp.where(row == 3, 1.0, jnp.where(row == 4, square, 0.0))
            )
            table_ref[cell] = own_stack(basis).astype(BF16)
            scaled_ref[cell] = own_stack(basis * own_inverse(own_ref, cell)).astype(BF16)
        return carry

    lax.fori_loop(0, CELLS // 4, some_cells, 0)


def kernel_and_slope(square):
    square = jnp.maximum(square, TINY)
    inverse = lax.rsqrt(square)
    dist = square * inverse
    left = jnp.maximum(1.0 - dist, 0.0)
    left_square = left * left
    near = square <= 0.25
    value = jnp.where(near, 0.5 - 3.0 * square * left, left_square * left)
    slope = jnp.where(near, 2.0 - 3.0 * dist, left_square * inverse)
    return value, slope


def slope_sixth(square):
    square = jnp.minimum(jnp.maximum(square, TINY), 1.0)
    inverse = lax.rsqrt(square)
    dist = square * inverse
    inner = 3.0 * dist - 2.0
    outer = (2.0 - dist) - inverse
    return jnp.where(square <= 0.25, inner, outer)


def together(begin, amount, first_half, second_half):
    def some_pairs(step, carry):
        for part in range(TOGETHER):
            first_half(step * TOGETHER + part, part)
        for part in range(TOGETHER):
            second_half(step * TOGETHER + part, part)
        return carry

    lax.fori_loop(begin // TOGETHER, amount // TOGETHER, some_pairs, 0)


def own_inverse(own_ref, owner):
    reach = own_ref[owner, 7:8, :]
    return 1.0 / (reach * reach)


def listed(which, info_ref, list_ref):
    pairs = info_ref.shape[1]

    def one_pair(pair, found):
        list_ref[found] = pair
        return found + (info_ref[2, pair] == which).astype(jnp.int32)

    found = lax.fori_loop(0, pairs, one_pair, jnp.int32(0))
    for spare in range(TOGETHER - 1):
        list_ref[found + spare] = pairs
    return (found + TOGETHER - 1) // TOGETHER * TOGETHER


def pair_at(list_ref, info_ref, shift_ref, place):
    pair = list_ref[place]
    real = pair < info_ref.shape[1]
    pair = jnp.minimum(pair, info_ref.shape[1] - 1)
    owner = info_ref[0, pair]
    shift = (shift_ref[0, pair], shift_ref[1, pair], shift_ref[2, pair])
    return owner, jnp.where(real, owner, CELLS), info_ref[1, pair], shift


def halves(value):
    first = rounded(value)
    return first, value - first


def split(value):
    high = value.astype(BF16)
    return high, (value - high.astype(F32)).astype(BF16)


def pair_scratch(pieces):
    return (
        [pltpu.VMEM((SLOTS, SLOTS), F32)] * TOGETHER
        + [pltpu.VMEM((8 * pieces, pieces * SLOTS), BF16)] * TOGETHER
        + [pltpu.VMEM((pieces * SLOTS, SLOTS), BF16)] * TOGETHER
    )


def add_sums(total_ref, line_ref, value_ref, target):
    total_ref[target] += lax.dot_general(
        line_ref[...], value_ref[...], NN, preferred_element_type=F32
    )


def near_pairs(begin, amount, scaled_ref, total_ref, refs, pair):
    squares, lines, values = (refs[i : i + TOGETHER] for i in range(0, 3 * TOGETHER, TOGETHER))

    def first_half(place, part):
        owner, _, block, shift = pair(place)
        row, seat, basis = far_basis(block, shift)
        squares[part][...] = lax.dot_general(
            far_stack(basis).astype(BF16), scaled_ref[owner], TN, preferred_element_type=F32
        )
        swirl = jnp.sum(seat[0:3] * block[4:7], axis=0, keepdims=True)
        side = jnp.where(
            row < 3, seat, jnp.where(row == 3, 1.0, jnp.where(row == 7, swirl, block))
        )
        first, second = halves(side * block[3:4])
        none = jnp.zeros((8, SLOTS), F32)
        lines[part][...] = jnp.concatenate(
            [
                jnp.concatenate([first, second, none, none], axis=0),
                jnp.concatenate([first, none, none, none], axis=0),
                jnp.concatenate([none, none, first, second], axis=0),
                jnp.concatenate([none, none, first, none], axis=0),
            ],
            axis=1,
        ).astype(BF16)

    def second_half(place, part):
        target = pair(place)[1]
        for start in range(0, SLOTS, STRIP):
            value, slope = kernel_and_slope(squares[part][start : start + STRIP, :])
            for piece, item in enumerate(split(slope) + split(value)):
                values[part][piece * SLOTS + start : piece * SLOTS + start + STRIP, :] = item
        add_sums(total_ref, lines[part], values[part], target)

    together(begin, amount, first_half, second_half)


def far_pairs(begin, amount, table_ref, total_ref, refs, pair):
    squares, lines, values = (refs[i : i + TOGETHER] for i in range(0, 3 * TOGETHER, TOGETHER))

    def first_half(place, part):
        owner, _, block, shift, factor = pair(place)
        row, seat, basis = far_basis(block, shift)
        reach = block[7:8]
        inverse = 1.0 / (reach * reach)
        squares[part][...] = lax.dot_general(
            far_stack(basis * inverse).astype(BF16),
            table_ref[owner],
            TN,
            preferred_element_type=F32,
        )
        side = jnp.where(row < 3, seat, jnp.where(row == 3, 1.0, 0.0))
        first, second = halves(
            side * (block[3:4] * factor * (6.0 * NORM) * inverse * inverse / reach)
        )
        none = jnp.zeros((8, SLOTS), F32)
        lines[part][...] = jnp.concatenate(
            [
                jnp.concatenate([first, second], axis=0),
                jnp.concatenate([first, none], axis=0),
            ],
            axis=1,
        ).astype(BF16)

    def second_half(place, part):
        target = pair(place)[1]
        for start in range(0, SLOTS, STRIP):
            slope = slope_sixth(squares[part][start : start + STRIP, :])
            for piece, item in enumerate(split(slope)):
                values[part][piece * SLOTS + start : piece * SLOTS + start + STRIP, :] = item
        add_sums(total_ref, lines[part], values[part], target)

    together(begin, amount, first_half, second_half)


def near_self_kernel(own_ref, scaled_ref, table_ref, total_ref, *refs):
    own_tables(own_ref, scaled_ref, table_ref)
    total_ref[...] = jnp.zeros_like(total_ref)
    near_pairs(
        0, CELLS, scaled_ref, total_ref, refs, lambda cell: (cell, cell, own_ref[cell], NO_SHIFT)
    )


def near_early_kernel(
    info_ref, shift_ref, scaled_ref, far_ref, before_ref, total_ref, list_ref, *refs
):
    amount = jnp.minimum(listed(0, info_ref, list_ref), EARLY)
    total_ref[...] = before_ref[...]

    def pair(place):
        owner, target, source, shift = pair_at(list_ref, info_ref, shift_ref, place)
        return owner, target, far_ref[source], shift

    near_pairs(0, amount, scaled_ref, total_ref, refs, pair)


def near_late_kernel(
    count_ref,
    info_ref,
    shift_ref,
    scaled_ref,
    far_a_ref,
    far_b_ref,
    before_ref,
    own_ref,
    heat_ref,
    total_ref,
    density_ref,
    factor_ref,
    list_ref,
    *refs,
):
    total_ref[...] = before_ref[...]
    for which, far_ref in enumerate((far_a_ref, far_b_ref)):
        amount = listed(which, info_ref, list_ref)

        def pair(place, far_ref=far_ref):
            owner, target, source, shift = pair_at(list_ref, info_ref, shift_ref, place)
            return owner, target, far_ref[source], shift

        near_pairs((EARLY, 0)[which], amount, scaled_ref, total_ref, refs, pair)
    lane = lax.broadcasted_iota(jnp.int32, (1, SLOTS), 1)

    def some_cells(step, carry):
        for part in range(4):
            cell = step * 4 + part
            line = pl.ds(cell, 1)
            raw = total_ref[cell, 19:20, :] + total_ref[cell, 27:28, :]
            reach = own_ref[cell, 7:8, :]
            raw = raw * (2.0 * NORM) / (reach * reach * reach)
            density = jnp.where(lane < count_ref[cell], raw, 1.0)
            density_ref[line, :] = density
            factor_ref[line, :] = 2.0 / 3.0 * heat_ref[line, :] / density
        return carry

    lax.fori_loop(0, CELLS // 4, some_cells, 0)


def far_self_kernel(own_ref, factor_ref, table_ref, total_ref, *refs):
    total_ref[...] = jnp.zeros_like(total_ref)

    def pair(cell):
        return cell, cell, own_ref[cell], NO_SHIFT, factor_ref[pl.ds(cell, 1), :]

    far_pairs(0, CELLS, table_ref, total_ref, refs, pair)


def far_cross_kernel(
    count_ref,
    info_ref,
    shift_ref,
    table_ref,
    own_ref,
    far_a_ref,
    far_b_ref,
    far_factor_ref,
    factor_ref,
    near_ref,
    before_ref,
    push_ref,
    total_ref,
    list_ref,
    *refs,
):
    total_ref[...] = before_ref[...]
    for which, far_ref in enumerate((far_a_ref, far_b_ref)):
        amount = listed(which, info_ref, list_ref)

        def pair(place, far_ref=far_ref):
            owner, target, source, shift = pair_at(list_ref, info_ref, shift_ref, place)
            line = info_ref[3, jnp.minimum(list_ref[place], info_ref.shape[1] - 1)]
            return owner, target, far_ref[source], shift, far_factor_ref[pl.ds(line, 1), :]

        far_pairs(0, amount, table_ref, total_ref, refs, pair)

    lane = lax.broadcasted_iota(jnp.int32, (1, SLOTS), 1)

    def some_cells(step, carry):
        for part in range(4):
            cell = step * 4 + part
            own = -(near_ref[cell, 0:8, :] + near_ref[cell, 8:16, :])
            far = total_ref[cell, 0:8, :] + total_ref[cell, 8:16, :]
            block = own_ref[cell]
            _, place = place_rows(block, NO_SHIFT)
            reach = block[7:8]
            inverse = 1.0 / (reach * reach)
            scale = factor_ref[pl.ds(cell, 1), :] * (6.0 * NORM) * inverse * inverse / reach
            place = place[0:3]
            speed = block[4:7]
            push = scale * (own[0:3] - place * own[3:4]) + (far[0:3] - place * far[3:4])
            warm = jnp.sum(
                speed * place * own[3:4] - speed * own[0:3] - place * own[4:7],
                axis=0,
                keepdims=True,
            )
            warm = scale * (warm + own[7:8])
            live = lane < count_ref[cell]
            push = jnp.where(live, push, 0.0)
            for line in range(3):
                push_ref[line, pl.ds(cell, 1), :] = push[line : line + 1]
            push_ref[3, pl.ds(cell, 1), :] = jnp.where(live, warm, 0.0)
        return carry

    lax.fori_loop(0, CELLS // 4, some_cells, 0)


def sort_kernel(owner_ref, cell_ref, mass_ref, mass_out, cell_out, parts_ref):
    span = 256
    together = 4
    devices = 128
    device_row = row_index((devices, span))
    slot_row = device_row.astype(F32)
    before = (
        row_index((span, span)) <= lax.broadcasted_iota(jnp.int32, (span, span), 1)
    ).astype(F32).astype(BF16)
    parts_ref[...] = jnp.zeros_like(parts_ref)

    def chunk(step, taken):
        named, values = [], []
        for part in range(together):
            line = pl.ds(step * together + part, 1)
            cell = cell_ref[line, :]
            chosen = device_row == owner_ref[line, :]
            ones = chosen.astype(F32)
            upto = lax.dot_general(ones.astype(BF16), before, NN, preferred_element_type=F32)
            rank = jnp.sum(ones * (upto + taken), axis=0, keepdims=True) - 1.0
            taken = taken + upto[:, span - 1 : span]
            named.append((slot_row == rank).astype(F32).astype(BF16))
            parts = thirds(mass_ref[line, :]) + (
                (cell & 63).astype(F32),
                ((cell >> 6) & 63).astype(F32),
                (cell >> 12).astype(F32),
            )
            values.append(
                jnp.concatenate([jnp.where(chosen, item, 0.0) for item in parts], axis=0).astype(BF16)
            )
        parts_ref[...] += lax.dot_general(
            jnp.concatenate(values, axis=1),
            jnp.concatenate(named, axis=1),
            NT,
            preferred_element_type=F32,
        )
        return taken

    lax.fori_loop(0, owner_ref.shape[0] // together, chunk, jnp.zeros((devices, 1), F32))
    n = devices
    mass_out[...] = (parts_ref[0:n] + parts_ref[n : 2 * n]) + parts_ref[2 * n : 3 * n]
    cell_out[...] = (
        parts_ref[3 * n : 4 * n]
        + 64.0 * parts_ref[4 * n : 5 * n]
        + 4096.0 * parts_ref[5 * n : 6 * n]
    )


def put_line(ref, line, rows):
    ref[pl.Slice(line, 128, 16), :] = rows[:, 0:128]
    ref[pl.Slice(8 + line, 128, 16), :] = rows[:, 128:256]


def get_line(ref, line):
    return jnp.concatenate(
        [ref[pl.Slice(line, 128, 16), :], ref[pl.Slice(8 + line, 128, 16), :]], axis=1
    )


def dot32(left, right):
    return lax.dot_general(left, right, NN, precision=highest, preferred_element_type=F32)


def deposit_kernel(mass_ref, cell_ref, z_ref, y_ref, out_ref, grid_ref):
    lanes = 128
    planes = grid_ref.shape[0]
    rows_at = row_index((planes, lanes))
    deep_at = row_index((M, lanes))
    grid_ref[...] = jnp.zeros_like(grid_ref)
    group = 8

    def chunk(step, carry):
        left, first, second = [], [], []
        for part in range(group):
            cell = cell_ref[pl.ds(step * group + part, 1), :].astype(jnp.int32)
            mass = mass_ref[pl.ds(step * group + part, 1), :]
            high = rounded(mass)
            low = mass - high
            left.append((rows_at == (cell >> 8)).astype(F32).astype(BF16))
            named = deep_at == (cell & 255)
            first.append(jnp.where(named, high, 0.0).astype(BF16))
            second.append(jnp.where(named, low, 0.0).astype(BF16))
        left = jnp.concatenate(left + left, axis=1)
        right = jnp.concatenate(first + second, axis=1)
        grid_ref[...] += lax.dot_general(left, right, NT, preferred_element_type=F32)
        return carry

    lax.fori_loop(0, mass_ref.shape[0] // group, chunk, 0)
    for plane in range(planes // M):
        piece = grid_ref[plane * M : (plane + 1) * M, :]
        turned = jnp.concatenate(
            [dot32(piece, z_ref[:, 0:M]), dot32(piece, z_ref[:, M : 2 * M])], axis=0
        )
        for part in range(4):
            rows = dot32(y_ref[part * 128 : (part + 1) * 128, :], turned)
            put_line(out_ref, plane * 4 + part, rows)


def filter_kernel(first_ref, in_ref, forward_ref, back_ref, out_ref):
    for line in range(2):
        pieces = [
            get_line(in_ref, plane * 4 + part * 2 + line)
            for part in range(2)
            for plane in range(2)
        ]
        spectrum = dot32(forward_ref[...], jnp.concatenate(pieces, axis=0))
        along_x = row_index((M, M))
        along_z = lax.broadcasted_iota(jnp.int32, (M, M), 1)
        along_x = jnp.where(along_x < M // 2, along_x, along_x - M)
        along_z = jnp.where(along_z < M // 2, along_z, along_z - M)
        along_y = first_ref[0] + line
        along_y = jnp.where(along_y < M // 2, along_y, along_y - M)
        square = (along_x * along_x + along_z * along_z + along_y * along_y).astype(F32)
        step = 2.0 * math.pi / M
        green = jnp.where(square > 0, -1.0 / (step * step * jnp.maximum(square, 1.0)), 0.0)
        spectrum = jnp.concatenate([spectrum[0:M] * green, spectrum[M : 2 * M] * green], axis=0)
        result = dot32(back_ref[...], spectrum)
        for piece in range(4):
            part, plane = piece // 2, piece % 2
            put_line(
                out_ref, plane * 4 + part * 2 + line, result[piece * 128 : (piece + 1) * 128]
            )


def potential_kernel(in_ref, y_ref, z_ref, out_ref):
    for plane in range(2):
        pieces = [get_line(in_ref, plane * 4 + part) for part in range(4)]
        turned = dot32(y_ref[...], jnp.concatenate(pieces, axis=0))
        out_ref[plane] = dot32(turned[0:M], z_ref[0:M, :]) + dot32(
            turned[M : 2 * M], z_ref[M : 2 * M, :]
        )


def wave_tables():
    index = np.arange(M)
    angle = 2.0 * np.pi / M * (np.outer(index, index) % M)
    cosine, sine = np.cos(angle), np.sin(angle)
    pairs = np.concatenate([index[0::2], index[1::2]])
    z_forward = np.concatenate([cosine, -sine], axis=1)
    y_forward = np.block([[cosine[pairs], sine[pairs]], [-sine[pairs], cosine[pairs]]])
    x_forward = np.block([[cosine[:, pairs], sine[:, pairs]], [-sine[:, pairs], cosine[:, pairs]]])
    x_back = np.block([[cosine[pairs], -sine[pairs]], [sine[pairs], cosine[pairs]]])
    y_back = np.block([[cosine[:, pairs], -sine[:, pairs]], [sine[:, pairs], cosine[:, pairs]]])
    z_back = np.concatenate([cosine, -sine], axis=0) / float(M) ** 3
    return [
        np.asarray(item, np.float32)
        for item in (z_forward, y_forward, x_forward, x_back, y_back, z_back)
    ]


def per_device(
    positions,
    velocities,
    masses,
    smoothing,
    energies,
    cell_counts,
    pair_list,
    export_list,
    mesh_owner,
    mesh_cell,
):
    devices = lax.axis_size("cells")
    me = lax.axis_index("cells").astype(jnp.int32)
    slots_iota = jnp.arange(SLOTS, dtype=jnp.int32)
    live = (slots_iota[None, :] < cell_counts[:, None]).astype(F32)
    heat = energies.reshape(CELLS, SLOTS)
    mass = masses.reshape(CELLS, SLOTS) * live
    own = jnp.concatenate(
        [
            positions.reshape(3, CELLS, SLOTS),
            (mass / SLOTS)[None],
            velocities.reshape(3, CELLS, SLOTS),
            smoothing.reshape(1, CELLS, SLOTS),
        ],
        axis=0,
    ).transpose(1, 0, 2)

    groups_a = [list(range(g, g + GROUP)) for g in range(0, devices, GROUP)]
    groups_b = [[(i + GROUP // 2) % devices for i in g] for g in groups_a]
    exports = export_list[0]
    lane32 = jnp.arange(GROUP, dtype=jnp.int32)

    def wanted(others):
        step = (me - others + devices // 2) % devices - devices // 2
        row = jnp.where(step < 0, step + HALF, step + HALF - 1)
        row = jnp.clip(row, 0, 2 * HALF - 1)
        return jnp.maximum(jnp.take(exports, row, axis=0), 0).reshape(-1)

    to_a = wanted(me // GROUP * GROUP + lane32)
    start_b = (me - GROUP // 2) % devices // GROUP * GROUP + GROUP // 2
    to_b = wanted((start_b + lane32) % devices)

    def swap(data, groups):
        return lax.all_to_all(data, "cells", 0, 0, axis_index_groups=groups, tiled=True)

    def pick(data, cells):
        return jnp.take(data, cells, axis=0, mode="clip")

    def after(data, *others):
        return lax.optimization_barrier((data, *others))[0]

    sent_a = pick(own, to_a)
    sent_b = pick(own, to_b)
    far_a = swap(sent_a, groups_a)
    mesh_owner, mesh_cell, mass = lax.optimization_barrier((mesh_owner, mesh_cell, mass, sent_a))[:3]

    owner_cell, neighbour, slot, direction = (pair_list[i] for i in range(4))
    step = jnp.where(neighbour < HALF, neighbour - HALF, neighbour - HALF + 1)
    other = (me + step) % devices
    in_a = other // GROUP == me // GROUP
    place = jnp.where(in_a, other % GROUP, (other - GROUP // 2) % GROUP)
    info = jnp.stack(
        [owner_cell, place * CAP + slot, jnp.where(in_a, 0, 1), other * CAP + slot]
    ).astype(jnp.int32)
    shift = jnp.stack([direction // 9 - 1, direction // 3 % 3 - 1, direction % 3 - 1]).astype(F32)

    lines = CELLS * SLOTS // 256
    mass_sent, cell_sent = pl.pallas_call(
        sort_kernel,
        out_shape=[jax.ShapeDtypeStruct((devices, 128), F32)] * 2,
        in_specs=[VMEM] * 3,
        out_specs=[VMEM] * 2,
        scratch_shapes=[pltpu.VMEM((6 * 128, 128), F32)],
        compiler_params=params(32),
        cost_estimate=cost(6e9, 1e6),
        name="sort_masses",
    )(mesh_owner.reshape(lines, 256), mesh_cell.reshape(lines, 256), mass.reshape(lines, 256))

    near_sums = jax.ShapeDtypeStruct((CELLS + 1, 32, SLOTS), F32)
    far_sums = jax.ShapeDtypeStruct((CELLS + 1, 16, SLOTS), F32)
    features = jax.ShapeDtypeStruct((CELLS, 48, SLOTS), BF16)
    each = jax.ShapeDtypeStruct((CELLS, SLOTS), F32)
    places = [pltpu.SMEM((256,), jnp.int32)]
    scaled, table, near = pl.pallas_call(
        near_self_kernel,
        out_shape=[features, features, near_sums],
        in_specs=[VMEM],
        out_specs=[VMEM] * 3,
        scratch_shapes=pair_scratch(4),
        compiler_params=params(48),
        cost_estimate=cost(8e9, 1e6),
        name="near_self",
    )(own)

    swapped = swap(after(jnp.stack([mass_sent, cell_sent], axis=1), far_a, near), None)
    far_b = swap(after(sent_b, swapped), groups_b)

    near = pl.pallas_call(
        near_early_kernel,
        out_shape=near_sums,
        in_specs=[SMEM] * 2 + [VMEM] * 3,
        out_specs=VMEM,
        scratch_shapes=places + pair_scratch(4),
        compiler_params=params(48),
        cost_estimate=cost(1.5e10, 1e6),
        name="near_early",
    )(info, shift, scaled, far_a, near)
    z_forward, y_forward, x_forward, x_back, y_back, z_back = wave_tables()
    wide = jax.ShapeDtypeStruct((devices * 16, M // 2), F32)
    half_way = pl.pallas_call(
        deposit_kernel,
        out_shape=wide,
        in_specs=[VMEM] * 4,
        out_specs=VMEM,
        scratch_shapes=[pltpu.VMEM((2 * M, M), F32)],
        compiler_params=params(48),
        cost_estimate=cost(1.5e10, 1e6),
        name="deposit",
    )(swapped[:, 0], swapped[:, 1], z_forward, y_forward)
    half_way = swap(after(half_way.reshape(devices, 16, M // 2), far_b, near), None)
    near, density, factor = pl.pallas_call(
        near_late_kernel,
        out_shape=[near_sums, each, each],
        in_specs=[SMEM] * 3 + [VMEM] * 6,
        out_specs=[VMEM] * 3,
        scratch_shapes=places + pair_scratch(4),
        compiler_params=params(48),
        cost_estimate=cost(1.5e10, 1e6),
        name="near_late",
    )(cell_counts, info, shift, scaled, far_a, far_b, near, own, heat)
    to_all = wanted(jnp.arange(devices, dtype=jnp.int32))
    far_factor = swap(after(pick(factor, to_all), half_way), None)

    far_total = pl.pallas_call(
        far_self_kernel,
        out_shape=far_sums,
        in_specs=[VMEM] * 3,
        out_specs=VMEM,
        scratch_shapes=pair_scratch(2),
        compiler_params=params(48),
        cost_estimate=cost(8e9, 1e6),
        name="far_self",
    )(own, factor, table)
    push = pl.pallas_call(
        far_cross_kernel,
        out_shape=jax.ShapeDtypeStruct((4, CELLS, SLOTS), F32),
        in_specs=[SMEM] * 3 + [VMEM] * 8,
        out_specs=VMEM,
        scratch_shapes=[pltpu.VMEM(far_sums.shape, F32)] + places + pair_scratch(2),
        compiler_params=params(48),
        cost_estimate=cost(3e10, 1e6),
        name="far_cross",
    )(cell_counts, info, shift, table, own, far_a, far_b, far_factor, factor, near, far_total)
    acceleration = push[0:3].reshape(3, -1)
    heating = push[3].reshape(-1)

    back = pl.pallas_call(
        filter_kernel,
        out_shape=wide,
        in_specs=[SMEM] + [VMEM] * 3,
        out_specs=VMEM,
        compiler_params=params(48),
        cost_estimate=cost(5e9, 1e6),
        name="filter",
    )((2 * me).reshape(1), half_way.reshape(devices * 16, M // 2), x_forward, x_back)
    back = swap(after(back.reshape(devices, 16, M // 2), far_factor, far_total), None)
    potential = pl.pallas_call(
        potential_kernel,
        out_shape=jax.ShapeDtypeStruct((2, M, M), F32),
        in_specs=[VMEM] * 3,
        out_specs=VMEM,
        compiler_params=params(48),
        cost_estimate=cost(4e9, 1e6),
        name="potential",
    )(back.reshape(devices * 16, M // 2), y_back, z_back)
    return (density.reshape(-1), acceleration, heating, potential)


def solution(mesh):
    in_specs = (
        P(None, "cells"),
        P(None, "cells"),
        P("cells"),
        P("cells"),
        P("cells"),
        P("cells"),
        P(None, "cells"),
        P("cells", None, None),
        P("cells", None),
        P("cells"),
    )
    out_specs = (P("cells"), P(None, "cells"), P("cells"), P("cells", None, None))
    return jax.shard_map(
        per_device, mesh=mesh, in_specs=in_specs, out_specs=out_specs, check_vma=False
    )
```

```python
import functools
import math

import jax
import jax.numpy as jnp
import numpy as np
from jax import lax
from jax.experimental import pallas as pl
from jax.experimental.pallas import tpu as pltpu
from jax.sharding import PartitionSpec as P

M = 256
GROUP = 32
CAP = 8
HALF = 13
CELLS = 32
SLOTS = 256
STRIP = 32
TOGETHER = 8
EARLY = 64
F32 = jnp.float32
BF16 = jnp.bfloat16
NORM = 8.0 / math.pi
TINY = 1e-30
VMEM = pl.BlockSpec(memory_space=pltpu.VMEM)
SMEM = pl.BlockSpec(memory_space=pltpu.SMEM)
NT = (((1,), (1,)), ((), ()))
NN = (((1,), (0,)), ((), ()))
TN = (((0,), (0,)), ((), ()))
NO_SHIFT = (0.0, 0.0, 0.0)
highest = lax.Precision.HIGHEST


def params(mib):
    return pltpu.CompilerParams(vmem_limit_bytes=mib * 1024 * 1024)


def cost(flops, nbytes):
    return pl.CostEstimate(
        flops=int(flops / 6), bytes_accessed=int(nbytes / 10), transcendentals=0
    )


def row_index(shape):
    return lax.broadcasted_iota(jnp.int32, shape, 0)


def rounded(value):
    return value.astype(BF16).astype(F32)


def thirds(value):
    first = rounded(value)
    rest = value - first
    second = rounded(rest)
    return first, second, rest - second


def place_rows(block, shift):
    row = row_index(block.shape)
    moved = jnp.where(row == 0, shift[0], jnp.where(row == 1, shift[1], shift[2])) - 0.5
    return row, jnp.where(row < 3, block + moved, 0.0)


def far_stack(basis):
    first, second, third = thirds(basis)
    return jnp.concatenate([first, second, first, second, third, first], axis=0)


def own_stack(basis):
    first, second, third = thirds(basis)
    return jnp.concatenate([first, first, second, second, first, third], axis=0)


def far_basis(block, shift):
    row, place = place_rows(block, shift)
    square = jnp.sum(place * place, axis=0, keepdims=True)
    basis = jnp.where(row == 3, square, jnp.where(row == 4, 1.0, place))
    return row, place, basis


def own_tables(own_ref, scaled_ref, table_ref):
    def some_cells(step, carry):
        for part in range(4):
            cell = step * 4 + part
            row, place = place_rows(own_ref[cell], NO_SHIFT)
            square = jnp.sum(place * place, axis=0, keepdims=True)
            basis = jnp.where(
                row < 3, -2.0 * place, jnp.where(row == 3, 1.0, jnp.where(row == 4, square, 0.0))
            )
            table_ref[cell] = own_stack(basis).astype(BF16)
            scaled_ref[cell] = own_stack(basis * own_inverse(own_ref, cell)).astype(BF16)
        return carry

    lax.fori_loop(0, CELLS // 4, some_cells, 0)


def kernel_and_slope(square):
    square = jnp.maximum(square, TINY)
    inverse = lax.rsqrt(square)
    dist = square * inverse
    left = jnp.maximum(1.0 - dist, 0.0)
    left_square = left * left
    near = square <= 0.25
    value = jnp.where(near, 0.5 - 3.0 * square * left, left_square * left)
    slope = jnp.where(near, 2.0 - 3.0 * dist, left_square * inverse)
    return value, slope


def slope_sixth(square):
    square = jnp.minimum(jnp.maximum(square, TINY), 1.0)
    inverse = lax.rsqrt(square)
    dist = square * inverse
    inner = 3.0 * dist - 2.0
    outer = (2.0 - dist) - inverse
    return jnp.where(square <= 0.25, inner, outer)


def together(begin, amount, first_half, second_half):
    def some_pairs(step, carry):
        for part in range(TOGETHER):
            first_half(step * TOGETHER + part, part)
        for part in range(TOGETHER):
            second_half(step * TOGETHER + part, part)
        return carry

    lax.fori_loop(begin // TOGETHER, amount // TOGETHER, some_pairs, 0)


def own_inverse(own_ref, owner):
    reach = own_ref[owner, 7:8, :]
    return 1.0 / (reach * reach)


def listed(which, info_ref, list_ref):
    pairs = info_ref.shape[1]

    def one_pair(pair, found):
        list_ref[found] = pair
        return found + (info_ref[2, pair] == which).astype(jnp.int32)

    found = lax.fori_loop(0, pairs, one_pair, jnp.int32(0))
    for spare in range(TOGETHER - 1):
        list_ref[found + spare] = pairs
    return (found + TOGETHER - 1) // TOGETHER * TOGETHER


def pair_at(list_ref, info_ref, shift_ref, place):
    pair = list_ref[place]
    real = pair < info_ref.shape[1]
    pair = jnp.minimum(pair, info_ref.shape[1] - 1)
    owner = info_ref[0, pair]
    shift = (shift_ref[0, pair], shift_ref[1, pair], shift_ref[2, pair])
    return owner, jnp.where(real, owner, CELLS), info_ref[1, pair], shift


def halves(value):
    first = rounded(value)
    return first, value - first


def split(value):
    high = value.astype(BF16)
    return high, (value - high.astype(F32)).astype(BF16)


def pair_scratch(pieces):
    return (
        [pltpu.VMEM((SLOTS, SLOTS), F32)] * TOGETHER
        + [pltpu.VMEM((8 * pieces, pieces * SLOTS), BF16)] * TOGETHER
        + [pltpu.VMEM((pieces * SLOTS, SLOTS), BF16)] * TOGETHER
    )


def add_sums(total_ref, line_ref, value_ref, target):
    total_ref[target] += lax.dot_general(
        line_ref[...], value_ref[...], NN, preferred_element_type=F32
    )


def near_pairs(begin, amount, scaled_ref, total_ref, refs, pair):
    squares, lines, values = (refs[i : i + TOGETHER] for i in range(0, 3 * TOGETHER, TOGETHER))

    def first_half(place, part):
        owner, _, block, shift = pair(place)
        row, seat, basis = far_basis(block, shift)
        squares[part][...] = lax.dot_general(
            far_stack(basis).astype(BF16), scaled_ref[owner], TN, preferred_element_type=F32
        )
        swirl = jnp.sum(seat[0:3] * block[4:7], axis=0, keepdims=True)
        side = jnp.where(
            row < 3, seat, jnp.where(row == 3, 1.0, jnp.where(row == 7, swirl, block))
        )
        first, second = halves(side * block[3:4])
        none = jnp.zeros((8, SLOTS), F32)
        lines[part][...] = jnp.concatenate(
            [
                jnp.concatenate([first, second, none, none], axis=0),
                jnp.concatenate([first, none, none, none], axis=0),
                jnp.concatenate([none, none, first, second], axis=0),
                jnp.concatenate([none, none, first, none], axis=0),
            ],
            axis=1,
        ).astype(BF16)

    def second_half(place, part):
        target = pair(place)[1]
        for start in range(0, SLOTS, STRIP):
            value, slope = kernel_and_slope(squares[part][start : start + STRIP, :])
            for piece, item in enumerate(split(slope) + split(value)):
                values[part][piece * SLOTS + start : piece * SLOTS + start + STRIP, :] = item
        add_sums(total_ref, lines[part], values[part], target)

    together(begin, amount, first_half, second_half)


def far_pairs(begin, amount, table_ref, total_ref, refs, pair):
    squares, lines, values = (refs[i : i + TOGETHER] for i in range(0, 3 * TOGETHER, TOGETHER))

    def first_half(place, part):
        owner, _, block, shift, factor = pair(place)
        row, seat, basis = far_basis(block, shift)
        reach = block[7:8]
        inverse = 1.0 / (reach * reach)
        squares[part][...] = lax.dot_general(
            far_stack(basis * inverse).astype(BF16),
            table_ref[owner],
            TN,
            preferred_element_type=F32,
        )
        side = jnp.where(row < 3, seat, jnp.where(row == 3, 1.0, 0.0))
        first, second = halves(
            side * (block[3:4] * factor * (6.0 * NORM) * inverse * inverse / reach)
        )
        none = jnp.zeros((8, SLOTS), F32)
        lines[part][...] = jnp.concatenate(
            [
                jnp.concatenate([first, second], axis=0),
                jnp.concatenate([first, none], axis=0),
            ],
            axis=1,
        ).astype(BF16)

    def second_half(place, part):
        target = pair(place)[1]
        for start in range(0, SLOTS, STRIP):
            slope = slope_sixth(squares[part][start : start + STRIP, :])
            for piece, item in enumerate(split(slope)):
                values[part][piece * SLOTS + start : piece * SLOTS + start + STRIP, :] = item
        add_sums(total_ref, lines[part], values[part], target)

    together(begin, amount, first_half, second_half)


def near_self_kernel(own_ref, scaled_ref, table_ref, total_ref, *refs):
    own_tables(own_ref, scaled_ref, table_ref)
    total_ref[...] = jnp.zeros_like(total_ref)
    near_pairs(
        0, CELLS, scaled_ref, total_ref, refs, lambda cell: (cell, cell, own_ref[cell], NO_SHIFT)
    )


def near_early_kernel(
    info_ref, shift_ref, scaled_ref, far_ref, before_ref, total_ref, list_ref, *refs
):
    amount = jnp.minimum(listed(0, info_ref, list_ref), EARLY)
    total_ref[...] = before_ref[...]

    def pair(place):
        owner, target, source, shift = pair_at(list_ref, info_ref, shift_ref, place)
        return owner, target, far_ref[source], shift

    near_pairs(0, amount, scaled_ref, total_ref, refs, pair)


def near_late_kernel(
    me_ref,
    export_ref,
    count_ref,
    info_ref,
    shift_ref,
    scaled_ref,
    far_a_ref,
    far_b_ref,
    before_ref,
    own_ref,
    heat_ref,
    total_ref,
    density_ref,
    factor_ref,
    sent_ref,
    list_ref,
    *refs,
):
    sent_ref[...] = jnp.zeros_like(sent_ref)
    total_ref[...] = before_ref[...]
    for which, far_ref in enumerate((far_a_ref, far_b_ref)):
        amount = listed(which, info_ref, list_ref)

        def pair(place, far_ref=far_ref):
            owner, target, source, shift = pair_at(list_ref, info_ref, shift_ref, place)
            return owner, target, far_ref[source], shift

        near_pairs((EARLY, 0)[which], amount, scaled_ref, total_ref, refs, pair)
    lane = lax.broadcasted_iota(jnp.int32, (1, SLOTS), 1)

    def some_cells(step, carry):
        for part in range(4):
            cell = step * 4 + part
            line = pl.ds(cell, 1)
            raw = total_ref[cell, 19:20, :] + total_ref[cell, 27:28, :]
            reach = own_ref[cell, 7:8, :]
            raw = raw * (2.0 * NORM) / (reach * reach * reach)
            density = jnp.where(lane < count_ref[cell], raw, 1.0)
            density_ref[line, :] = density
            factor_ref[line, :] = 2.0 / 3.0 * heat_ref[line, :] / density
        return carry

    lax.fori_loop(0, CELLS // 4, some_cells, 0)

    def one_peer(peer, carry):
        cells = [jnp.maximum(export_ref[peer, slot], 0) for slot in range(CAP)]
        sent_ref[receiver(peer, me_ref[0], sent_ref.shape[0])] = jnp.concatenate(
            [factor_ref[pl.ds(cell, 1), :] for cell in cells], axis=0
        )
        return carry

    lax.fori_loop(0, 2 * HALF, one_peer, 0)


def far_self_kernel(own_ref, factor_ref, table_ref, total_ref, *refs):
    total_ref[...] = jnp.zeros_like(total_ref)

    def pair(cell):
        return cell, cell, own_ref[cell], NO_SHIFT, factor_ref[pl.ds(cell, 1), :]

    far_pairs(0, CELLS, table_ref, total_ref, refs, pair)


def far_cross_kernel(
    count_ref,
    info_ref,
    shift_ref,
    table_ref,
    own_ref,
    far_a_ref,
    far_b_ref,
    far_factor_ref,
    factor_ref,
    near_ref,
    before_ref,
    push_ref,
    total_ref,
    list_ref,
    *refs,
):
    total_ref[...] = before_ref[...]
    for which, far_ref in enumerate((far_a_ref, far_b_ref)):
        amount = listed(which, info_ref, list_ref)

        def pair(place, far_ref=far_ref):
            owner, target, source, shift = pair_at(list_ref, info_ref, shift_ref, place)
            line = info_ref[3, jnp.minimum(list_ref[place], info_ref.shape[1] - 1)]
            return owner, target, far_ref[source], shift, far_factor_ref[pl.ds(line, 1), :]

        far_pairs(0, amount, table_ref, total_ref, refs, pair)

    lane = lax.broadcasted_iota(jnp.int32, (1, SLOTS), 1)

    def some_cells(step, carry):
        for part in range(4):
            cell = step * 4 + part
            own = -(near_ref[cell, 0:8, :] + near_ref[cell, 8:16, :])
            far = total_ref[cell, 0:8, :] + total_ref[cell, 8:16, :]
            block = own_ref[cell]
            _, place = place_rows(block, NO_SHIFT)
            reach = block[7:8]
            inverse = 1.0 / (reach * reach)
            scale = factor_ref[pl.ds(cell, 1), :] * (6.0 * NORM) * inverse * inverse / reach
            place = place[0:3]
            speed = block[4:7]
            push = scale * (own[0:3] - place * own[3:4]) + (far[0:3] - place * far[3:4])
            warm = jnp.sum(
                speed * place * own[3:4] - speed * own[0:3] - place * own[4:7],
                axis=0,
                keepdims=True,
            )
            warm = scale * (warm + own[7:8])
            live = lane < count_ref[cell]
            push = jnp.where(live, push, 0.0)
            for line in range(3):
                push_ref[line, pl.ds(cell, 1), :] = push[line : line + 1]
            push_ref[3, pl.ds(cell, 1), :] = jnp.where(live, warm, 0.0)
        return carry

    lax.fori_loop(0, CELLS // 4, some_cells, 0)


def receiver(peer, me, devices):
    step = jnp.where(peer < HALF, peer - HALF, peer - HALF + 1)
    return lax.rem(me - step + devices, devices)


def export_kernel(
    devices,
    me_ref,
    export_ref,
    count_ref,
    place_ref,
    speed_ref,
    mass_ref,
    reach_ref,
    own_ref,
    live_ref,
    sent_a_ref,
    sent_b_ref,
):
    lane = lax.broadcasted_iota(jnp.int32, (1, SLOTS), 1)

    def some_cells(step, carry):
        for part in range(4):
            cell = step * 4 + part
            line = pl.ds(cell, 1)
            lanes = pl.ds(pl.multiple_of(cell * SLOTS, SLOTS), SLOTS)
            mass = jnp.where(lane < count_ref[cell], mass_ref[line, :], 0.0)
            live_ref[line, :] = mass
            own_ref[cell] = jnp.concatenate(
                [place_ref[:, lanes], mass / SLOTS, speed_ref[:, lanes], reach_ref[line, :]], axis=0
            )
        return carry

    lax.fori_loop(0, CELLS // 4, some_cells, 0)
    me = me_ref[0]

    def one_peer(peer, carry):
        target = receiver(peer, me, devices)
        same = target // GROUP == me // GROUP
        seat_a = lax.rem(target, GROUP) * CAP
        seat_b = lax.rem(target + devices - GROUP // 2, GROUP) * CAP

        @pl.when(same)
        def _():
            for slot in range(CAP):
                sent_a_ref[seat_a + slot] = own_ref[jnp.maximum(export_ref[peer, slot], 0)]

        @pl.when(jnp.logical_not(same))
        def _():
            for slot in range(CAP):
                sent_b_ref[seat_b + slot] = own_ref[jnp.maximum(export_ref[peer, slot], 0)]

        return carry

    lax.fori_loop(0, 2 * HALF, one_peer, 0)


def sort_kernel(owner_ref, cell_ref, mass_ref, mass_out, cell_out, parts_ref):
    span = 256
    together = 4
    devices = 128
    device_row = row_index((devices, span))
    slot_row = device_row.astype(F32)
    before = (
        row_index((span, span)) <= lax.broadcasted_iota(jnp.int32, (span, span), 1)
    ).astype(F32).astype(BF16)
    parts_ref[...] = jnp.zeros_like(parts_ref)

    def chunk(step, taken):
        named, values = [], []
        for part in range(together):
            line = pl.ds(step * together + part, 1)
            cell = cell_ref[line, :]
            chosen = device_row == owner_ref[line, :]
            ones = chosen.astype(F32)
            upto = lax.dot_general(ones.astype(BF16), before, NN, preferred_element_type=F32)
            rank = jnp.sum(ones * (upto + taken), axis=0, keepdims=True) - 1.0
            taken = taken + upto[:, span - 1 : span]
            named.append((slot_row == rank).astype(F32).astype(BF16))
            parts = thirds(mass_ref[line, :]) + (
                (cell & 63).astype(F32),
                ((cell >> 6) & 63).astype(F32),
                (cell >> 12).astype(F32),
            )
            values.append(
                jnp.concatenate([jnp.where(chosen, item, 0.0) for item in parts], axis=0).astype(BF16)
            )
        parts_ref[...] += lax.dot_general(
            jnp.concatenate(values, axis=1),
            jnp.concatenate(named, axis=1),
            NT,
            preferred_element_type=F32,
        )
        return taken

    lax.fori_loop(0, owner_ref.shape[0] // together, chunk, jnp.zeros((devices, 1), F32))
    n = devices
    mass_out[...] = (parts_ref[0:n] + parts_ref[n : 2 * n]) + parts_ref[2 * n : 3 * n]
    cell_out[...] = (
        parts_ref[3 * n : 4 * n]
        + 64.0 * parts_ref[4 * n : 5 * n]
        + 4096.0 * parts_ref[5 * n : 6 * n]
    )


def put_line(ref, line, rows):
    ref[pl.Slice(line, 128, 16), :] = rows[:, 0:128]
    ref[pl.Slice(8 + line, 128, 16), :] = rows[:, 128:256]


def get_line(ref, line):
    return jnp.concatenate(
        [ref[pl.Slice(line, 128, 16), :], ref[pl.Slice(8 + line, 128, 16), :]], axis=1
    )


def dot32(left, right):
    return lax.dot_general(left, right, NN, precision=highest, preferred_element_type=F32)


def deposit_kernel(mass_ref, cell_ref, z_ref, y_ref, out_ref, grid_ref):
    lanes = 128
    planes = grid_ref.shape[0]
    rows_at = row_index((planes, lanes))
    deep_at = row_index((M, lanes))
    grid_ref[...] = jnp.zeros_like(grid_ref)
    group = 8

    def chunk(step, carry):
        left, first, second = [], [], []
        for part in range(group):
            cell = cell_ref[pl.ds(step * group + part, 1), :].astype(jnp.int32)
            mass = mass_ref[pl.ds(step * group + part, 1), :]
            high = rounded(mass)
            low = mass - high
            left.append((rows_at == (cell >> 8)).astype(F32).astype(BF16))
            named = deep_at == (cell & 255)
            first.append(jnp.where(named, high, 0.0).astype(BF16))
            second.append(jnp.where(named, low, 0.0).astype(BF16))
        left = jnp.concatenate(left + left, axis=1)
        right = jnp.concatenate(first + second, axis=1)
        grid_ref[...] += lax.dot_general(left, right, NT, preferred_element_type=F32)
        return carry

    lax.fori_loop(0, mass_ref.shape[0] // group, chunk, 0)
    for plane in range(planes // M):
        piece = grid_ref[plane * M : (plane + 1) * M, :]
        turned = jnp.concatenate(
            [dot32(piece, z_ref[:, 0:M]), dot32(piece, z_ref[:, M : 2 * M])], axis=0
        )
        for part in range(4):
            rows = dot32(y_ref[part * 128 : (part + 1) * 128, :], turned)
            put_line(out_ref, plane * 4 + part, rows)


def filter_kernel(first_ref, in_ref, forward_ref, back_ref, out_ref):
    for line in range(2):
        pieces = [
            get_line(in_ref, plane * 4 + part * 2 + line)
            for part in range(2)
            for plane in range(2)
        ]
        spectrum = dot32(forward_ref[...], jnp.concatenate(pieces, axis=0))
        along_x = row_index((M, M))
        along_z = lax.broadcasted_iota(jnp.int32, (M, M), 1)
        along_x = jnp.where(along_x < M // 2, along_x, along_x - M)
        along_z = jnp.where(along_z < M // 2, along_z, along_z - M)
        along_y = first_ref[0] + line
        along_y = jnp.where(along_y < M // 2, along_y, along_y - M)
        square = (along_x * along_x + along_z * along_z + along_y * along_y).astype(F32)
        step = 2.0 * math.pi / M
        green = jnp.where(square > 0, -1.0 / (step * step * jnp.maximum(square, 1.0)), 0.0)
        spectrum = jnp.concatenate([spectrum[0:M] * green, spectrum[M : 2 * M] * green], axis=0)
        result = dot32(back_ref[...], spectrum)
        for piece in range(4):
            part, plane = piece // 2, piece % 2
            put_line(
                out_ref, plane * 4 + part * 2 + line, result[piece * 128 : (piece + 1) * 128]
            )


def potential_kernel(in_ref, y_ref, z_ref, out_ref):
    for plane in range(2):
        pieces = [get_line(in_ref, plane * 4 + part) for part in range(4)]
        turned = dot32(y_ref[...], jnp.concatenate(pieces, axis=0))
        out_ref[plane] = dot32(turned[0:M], z_ref[0:M, :]) + dot32(
            turned[M : 2 * M], z_ref[M : 2 * M, :]
        )


def wave_tables():
    index = np.arange(M)
    angle = 2.0 * np.pi / M * (np.outer(index, index) % M)
    cosine, sine = np.cos(angle), np.sin(angle)
    pairs = np.concatenate([index[0::2], index[1::2]])
    z_forward = np.concatenate([cosine, -sine], axis=1)
    y_forward = np.block([[cosine[pairs], sine[pairs]], [-sine[pairs], cosine[pairs]]])
    x_forward = np.block([[cosine[:, pairs], sine[:, pairs]], [-sine[:, pairs], cosine[:, pairs]]])
    x_back = np.block([[cosine[pairs], -sine[pairs]], [sine[pairs], cosine[pairs]]])
    y_back = np.block([[cosine[:, pairs], -sine[:, pairs]], [sine[:, pairs], cosine[:, pairs]]])
    z_back = np.concatenate([cosine, -sine], axis=0) / float(M) ** 3
    return [
        np.asarray(item, np.float32)
        for item in (z_forward, y_forward, x_forward, x_back, y_back, z_back)
    ]


def per_device(
    positions,
    velocities,
    masses,
    smoothing,
    energies,
    cell_counts,
    pair_list,
    export_list,
    mesh_owner,
    mesh_cell,
):
    devices = lax.axis_size("cells")
    me = lax.axis_index("cells").astype(jnp.int32)
    heat = energies.reshape(CELLS, SLOTS)

    groups_a = [list(range(g, g + GROUP)) for g in range(0, devices, GROUP)]
    groups_b = [[(i + GROUP // 2) % devices for i in g] for g in groups_a]
    def swap(data, groups):
        return lax.all_to_all(data, "cells", 0, 0, axis_index_groups=groups, tiled=True)

    def after(data, *others):
        return lax.optimization_barrier((data, *others))[0]

    exports = export_list[0]
    here = me.reshape(1)
    sent = jax.ShapeDtypeStruct((GROUP * CAP, 8, SLOTS), F32)
    own, mass, sent_a, sent_b = pl.pallas_call(
        functools.partial(export_kernel, devices),
        out_shape=[
            jax.ShapeDtypeStruct((CELLS, 8, SLOTS), F32),
            jax.ShapeDtypeStruct((CELLS, SLOTS), F32),
            sent,
            sent,
        ],
        in_specs=[SMEM] * 3 + [VMEM] * 4,
        out_specs=[VMEM] * 4,
        compiler_params=params(32),
        cost_estimate=cost(2e9, 5e6),
        name="exports",
    )(
        here,
        exports,
        cell_counts,
        positions,
        velocities,
        masses.reshape(CELLS, SLOTS),
        smoothing.reshape(CELLS, SLOTS),
    )
    far_a = swap(sent_a, groups_a)
    mesh_owner, mesh_cell, mass = lax.optimization_barrier((mesh_owner, mesh_cell, mass, sent_a))[:3]

    owner_cell, neighbour, slot, direction = (pair_list[i] for i in range(4))
    step = jnp.where(neighbour < HALF, neighbour - HALF, neighbour - HALF + 1)
    other = (me + step) % devices
    in_a = other // GROUP == me // GROUP
    place = jnp.where(in_a, other % GROUP, (other - GROUP // 2) % GROUP)
    info = jnp.stack(
        [owner_cell, place * CAP + slot, jnp.where(in_a, 0, 1), other * CAP + slot]
    ).astype(jnp.int32)
    shift = jnp.stack([direction // 9 - 1, direction // 3 % 3 - 1, direction % 3 - 1]).astype(F32)

    lines = CELLS * SLOTS // 256
    mass_sent, cell_sent = pl.pallas_call(
        sort_kernel,
        out_shape=[jax.ShapeDtypeStruct((devices, 128), F32)] * 2,
        in_specs=[VMEM] * 3,
        out_specs=[VMEM] * 2,
        scratch_shapes=[pltpu.VMEM((6 * 128, 128), F32)],
        compiler_params=params(32),
        cost_estimate=cost(6e9, 1e6),
        name="sort_masses",
    )(mesh_owner.reshape(lines, 256), mesh_cell.reshape(lines, 256), mass.reshape(lines, 256))

    near_sums = jax.ShapeDtypeStruct((CELLS + 1, 32, SLOTS), F32)
    far_sums = jax.ShapeDtypeStruct((CELLS + 1, 16, SLOTS), F32)
    features = jax.ShapeDtypeStruct((CELLS, 48, SLOTS), BF16)
    each = jax.ShapeDtypeStruct((CELLS, SLOTS), F32)
    places = [pltpu.SMEM((256,), jnp.int32)]
    scaled, table, near = pl.pallas_call(
        near_self_kernel,
        out_shape=[features, features, near_sums],
        in_specs=[VMEM],
        out_specs=[VMEM] * 3,
        scratch_shapes=pair_scratch(4),
        compiler_params=params(48),
        cost_estimate=cost(8e9, 1e6),
        name="near_self",
    )(own)

    swapped = swap(after(jnp.stack([mass_sent, cell_sent], axis=1), far_a, near), None)
    far_b = swap(after(sent_b, swapped), groups_b)

    near = pl.pallas_call(
        near_early_kernel,
        out_shape=near_sums,
        in_specs=[SMEM] * 2 + [VMEM] * 3,
        out_specs=VMEM,
        scratch_shapes=places + pair_scratch(4),
        compiler_params=params(48),
        cost_estimate=cost(1.5e10, 1e6),
        name="near_early",
    )(info, shift, scaled, far_a, near)
    z_forward, y_forward, x_forward, x_back, y_back, z_back = wave_tables()
    wide = jax.ShapeDtypeStruct((devices * 16, M // 2), F32)
    half_way = pl.pallas_call(
        deposit_kernel,
        out_shape=wide,
        in_specs=[VMEM] * 4,
        out_specs=VMEM,
        scratch_shapes=[pltpu.VMEM((2 * M, M), F32)],
        compiler_params=params(48),
        cost_estimate=cost(1.5e10, 1e6),
        name="deposit",
    )(swapped[:, 0], swapped[:, 1], z_forward, y_forward)
    half_way = swap(after(half_way.reshape(devices, 16, M // 2), far_b, near), None)
    near, density, factor, sent_factor = pl.pallas_call(
        near_late_kernel,
        out_shape=[near_sums, each, each, jax.ShapeDtypeStruct((devices, CAP, SLOTS), F32)],
        in_specs=[SMEM] * 5 + [VMEM] * 6,
        out_specs=[VMEM] * 4,
        scratch_shapes=places + pair_scratch(4),
        compiler_params=params(48),
        cost_estimate=cost(1.5e10, 1e6),
        name="near_late",
    )(here, exports, cell_counts, info, shift, scaled, far_a, far_b, near, own, heat)
    far_factor = swap(after(sent_factor, half_way), None).reshape(devices * CAP, SLOTS)

    far_total = pl.pallas_call(
        far_self_kernel,
        out_shape=far_sums,
        in_specs=[VMEM] * 3,
        out_specs=VMEM,
        scratch_shapes=pair_scratch(2),
        compiler_params=params(48),
        cost_estimate=cost(8e9, 1e6),
        name="far_self",
    )(own, factor, table)
    push = pl.pallas_call(
        far_cross_kernel,
        out_shape=jax.ShapeDtypeStruct((4, CELLS, SLOTS), F32),
        in_specs=[SMEM] * 3 + [VMEM] * 8,
        out_specs=VMEM,
        scratch_shapes=[pltpu.VMEM(far_sums.shape, F32)] + places + pair_scratch(2),
        compiler_params=params(48),
        cost_estimate=cost(3e10, 1e6),
        name="far_cross",
    )(cell_counts, info, shift, table, own, far_a, far_b, far_factor, factor, near, far_total)
    acceleration = push[0:3].reshape(3, -1)
    heating = push[3].reshape(-1)

    back = pl.pallas_call(
        filter_kernel,
        out_shape=wide,
        in_specs=[SMEM] + [VMEM] * 3,
        out_specs=VMEM,
        compiler_params=params(48),
        cost_estimate=cost(5e9, 1e6),
        name="filter",
    )((2 * me).reshape(1), half_way.reshape(devices * 16, M // 2), x_forward, x_back)
    back = swap(after(back.reshape(devices, 16, M // 2), far_factor, far_total), None)
    potential = pl.pallas_call(
        potential_kernel,
        out_shape=jax.ShapeDtypeStruct((2, M, M), F32),
        in_specs=[VMEM] * 3,
        out_specs=VMEM,
        compiler_params=params(48),
        cost_estimate=cost(4e9, 1e6),
        name="potential",
    )(back.reshape(devices * 16, M // 2), y_back, z_back)
    return (density.reshape(-1), acceleration, heating, potential)


def solution(mesh):
    in_specs = (
        P(None, "cells"),
        P(None, "cells"),
        P("cells"),
        P("cells"),
        P("cells"),
        P("cells"),
        P(None, "cells"),
        P("cells", None, None),
        P("cells", None),
        P("cells"),
    )
    out_specs = (P("cells"), P(None, "cells"), P("cells"), P("cells", None, None))
    return jax.shard_map(
        per_device, mesh=mesh, in_specs=in_specs, out_specs=out_specs, check_vma=False
    )
```

```python
import functools
import math

import jax
import jax.numpy as jnp
import numpy as np
from jax import lax
from jax.experimental import pallas as pl
from jax.experimental.pallas import tpu as pltpu
from jax.sharding import PartitionSpec as P

M = 256
GROUP = 32
CAP = 8
HALF = 13
CELLS = 32
SLOTS = 256
STRIP = 32
TOGETHER = 8
EARLY = 64
F32 = jnp.float32
BF16 = jnp.bfloat16
NORM = 8.0 / math.pi
TINY = 1e-30
VMEM = pl.BlockSpec(memory_space=pltpu.VMEM)
SMEM = pl.BlockSpec(memory_space=pltpu.SMEM)
NT = (((1,), (1,)), ((), ()))
NN = (((1,), (0,)), ((), ()))
TN = (((0,), (0,)), ((), ()))
NO_SHIFT = (0.0, 0.0, 0.0)
highest = lax.Precision.HIGHEST


def params(mib):
    return pltpu.CompilerParams(vmem_limit_bytes=mib * 1024 * 1024)


def cost(flops, nbytes):
    return pl.CostEstimate(
        flops=int(flops / 6), bytes_accessed=int(nbytes / 10), transcendentals=0
    )


def row_index(shape):
    return lax.broadcasted_iota(jnp.int32, shape, 0)


def rounded(value):
    return value.astype(BF16).astype(F32)


def thirds(value):
    first = rounded(value)
    rest = value - first
    second = rounded(rest)
    return first, second, rest - second


def place_rows(block, shift):
    row = row_index(block.shape)
    moved = jnp.where(row == 0, shift[0], jnp.where(row == 1, shift[1], shift[2])) - 0.5
    return row, jnp.where(row < 3, block + moved, 0.0)


def far_stack(basis):
    first, second, third = thirds(basis)
    return jnp.concatenate([first, second, first, second, third, first], axis=0)


def own_stack(basis):
    first, second, third = thirds(basis)
    return jnp.concatenate([first, first, second, second, first, third], axis=0)


def far_basis(block, shift):
    row, place = place_rows(block, shift)
    square = jnp.sum(place * place, axis=0, keepdims=True)
    basis = jnp.where(row == 3, square, jnp.where(row == 4, 1.0, place))
    return row, place, basis


def own_tables(own_ref, scaled_ref, table_ref):
    def some_cells(step, carry):
        for part in range(4):
            cell = step * 4 + part
            row, place = place_rows(own_ref[cell], NO_SHIFT)
            square = jnp.sum(place * place, axis=0, keepdims=True)
            basis = jnp.where(
                row < 3, -2.0 * place, jnp.where(row == 3, 1.0, jnp.where(row == 4, square, 0.0))
            )
            table_ref[cell] = own_stack(basis).astype(BF16)
            scaled_ref[cell] = own_stack(basis * own_inverse(own_ref, cell)).astype(BF16)
        return carry

    lax.fori_loop(0, CELLS // 4, some_cells, 0)


def kernel_and_slope(square):
    square = jnp.maximum(square, TINY)
    inverse = lax.rsqrt(square)
    dist = square * inverse
    left = jnp.maximum(1.0 - dist, 0.0)
    left_square = left * left
    near = square <= 0.25
    value = jnp.where(near, 0.5 - 3.0 * square * left, left_square * left)
    slope = jnp.where(near, 2.0 - 3.0 * dist, left_square * inverse)
    return value, slope


def slope_sixth(square):
    square = jnp.minimum(jnp.maximum(square, TINY), 1.0)
    inverse = lax.rsqrt(square)
    dist = square * inverse
    inner = 3.0 * dist - 2.0
    outer = (2.0 - dist) - inverse
    return jnp.where(square <= 0.25, inner, outer)


def together(begin, amount, first_half, second_half):
    def some_pairs(step, carry):
        for part in range(TOGETHER):
            first_half(step * TOGETHER + part, part)
        for part in range(TOGETHER):
            second_half(step * TOGETHER + part, part)
        return carry

    lax.fori_loop(begin // TOGETHER, amount // TOGETHER, some_pairs, 0)


def own_inverse(own_ref, owner):
    reach = own_ref[owner, 7:8, :]
    return 1.0 / (reach * reach)


def listed(which, info_ref, list_ref):
    pairs = info_ref.shape[1]

    def one_pair(pair, found):
        list_ref[found] = pair
        return found + (info_ref[2, pair] == which).astype(jnp.int32)

    found = lax.fori_loop(0, pairs, one_pair, jnp.int32(0))
    for spare in range(TOGETHER - 1):
        list_ref[found + spare] = pairs
    return (found + TOGETHER - 1) // TOGETHER * TOGETHER


def pair_at(list_ref, info_ref, shift_ref, place):
    pair = list_ref[place]
    real = pair < info_ref.shape[1]
    pair = jnp.minimum(pair, info_ref.shape[1] - 1)
    owner = info_ref[0, pair]
    shift = (shift_ref[0, pair], shift_ref[1, pair], shift_ref[2, pair])
    return owner, jnp.where(real, owner, CELLS), info_ref[1, pair], shift


def halves(value):
    first = rounded(value)
    return first, value - first


def split(value):
    high = value.astype(BF16)
    return high, (value - high.astype(F32)).astype(BF16)


def pair_scratch(pieces):
    return (
        [pltpu.VMEM((SLOTS, SLOTS), F32)] * TOGETHER
        + [pltpu.VMEM((8 * pieces, pieces * SLOTS), BF16)] * TOGETHER
        + [pltpu.VMEM((pieces * SLOTS, SLOTS), BF16)] * TOGETHER
    )


def add_sums(total_ref, line_ref, value_ref, target):
    total_ref[target] += lax.dot_general(
        line_ref[...], value_ref[...], NN, preferred_element_type=F32
    )


def near_pairs(begin, amount, scaled_ref, total_ref, refs, pair):
    squares, lines, values = (refs[i : i + TOGETHER] for i in range(0, 3 * TOGETHER, TOGETHER))

    def first_half(place, part):
        owner, _, block, shift = pair(place)
        row, seat, basis = far_basis(block, shift)
        squares[part][...] = lax.dot_general(
            far_stack(basis).astype(BF16), scaled_ref[owner], TN, preferred_element_type=F32
        )
        swirl = jnp.sum(seat[0:3] * block[4:7], axis=0, keepdims=True)
        side = jnp.where(
            row < 3, seat, jnp.where(row == 3, 1.0, jnp.where(row == 7, swirl, block))
        )
        first, second = halves(side * block[3:4])
        none = jnp.zeros((8, SLOTS), F32)
        lines[part][...] = jnp.concatenate(
            [
                jnp.concatenate([first, second, none, none], axis=0),
                jnp.concatenate([first, none, none, none], axis=0),
                jnp.concatenate([none, none, first, second], axis=0),
                jnp.concatenate([none, none, first, none], axis=0),
            ],
            axis=1,
        ).astype(BF16)

    def second_half(place, part):
        target = pair(place)[1]
        for start in range(0, SLOTS, STRIP):
            value, slope = kernel_and_slope(squares[part][start : start + STRIP, :])
            for piece, item in enumerate(split(slope) + split(value)):
                values[part][piece * SLOTS + start : piece * SLOTS + start + STRIP, :] = item
        add_sums(total_ref, lines[part], values[part], target)

    together(begin, amount, first_half, second_half)


def far_pairs(begin, amount, table_ref, total_ref, refs, pair):
    squares, lines, values = (refs[i : i + TOGETHER] for i in range(0, 3 * TOGETHER, TOGETHER))

    def first_half(place, part):
        owner, _, block, shift, factor = pair(place)
        row, seat, basis = far_basis(block, shift)
        reach = block[7:8]
        inverse = 1.0 / (reach * reach)
        squares[part][...] = lax.dot_general(
            far_stack(basis * inverse).astype(BF16),
            table_ref[owner],
            TN,
            preferred_element_type=F32,
        )
        side = jnp.where(row < 3, seat, jnp.where(row == 3, 1.0, 0.0))
        first, second = halves(
            side * (block[3:4] * factor * (6.0 * NORM) * inverse * inverse / reach)
        )
        none = jnp.zeros((8, SLOTS), F32)
        lines[part][...] = jnp.concatenate(
            [
                jnp.concatenate([first, second], axis=0),
                jnp.concatenate([first, none], axis=0),
            ],
            axis=1,
        ).astype(BF16)

    def second_half(place, part):
        target = pair(place)[1]
        for start in range(0, SLOTS, STRIP):
            slope = slope_sixth(squares[part][start : start + STRIP, :])
            for piece, item in enumerate(split(slope)):
                values[part][piece * SLOTS + start : piece * SLOTS + start + STRIP, :] = item
        add_sums(total_ref, lines[part], values[part], target)

    together(begin, amount, first_half, second_half)


def near_self_kernel(own_ref, scaled_ref, table_ref, total_ref, *refs):
    own_tables(own_ref, scaled_ref, table_ref)
    total_ref[...] = jnp.zeros_like(total_ref)
    near_pairs(
        0, CELLS, scaled_ref, total_ref, refs, lambda cell: (cell, cell, own_ref[cell], NO_SHIFT)
    )


def near_early_kernel(
    info_ref, shift_ref, scaled_ref, far_ref, before_ref, total_ref, list_ref, *refs
):
    amount = jnp.minimum(listed(0, info_ref, list_ref), EARLY)
    total_ref[...] = before_ref[...]

    def pair(place):
        owner, target, source, shift = pair_at(list_ref, info_ref, shift_ref, place)
        return owner, target, far_ref[source], shift

    near_pairs(0, amount, scaled_ref, total_ref, refs, pair)


def near_late_kernel(
    me_ref,
    export_ref,
    count_ref,
    info_ref,
    shift_ref,
    scaled_ref,
    far_a_ref,
    far_b_ref,
    before_ref,
    own_ref,
    heat_ref,
    total_ref,
    density_ref,
    factor_ref,
    sent_ref,
    list_ref,
    *refs,
):
    sent_ref[...] = jnp.zeros_like(sent_ref)
    total_ref[...] = before_ref[...]
    for which, far_ref in enumerate((far_a_ref, far_b_ref)):
        amount = listed(which, info_ref, list_ref)

        def pair(place, far_ref=far_ref):
            owner, target, source, shift = pair_at(list_ref, info_ref, shift_ref, place)
            return owner, target, far_ref[source], shift

        near_pairs((EARLY, 0)[which], amount, scaled_ref, total_ref, refs, pair)
    lane = lax.broadcasted_iota(jnp.int32, (1, SLOTS), 1)

    def some_cells(step, carry):
        for part in range(4):
            cell = step * 4 + part
            line = pl.ds(cell, 1)
            raw = total_ref[cell, 19:20, :] + total_ref[cell, 27:28, :]
            reach = own_ref[cell, 7:8, :]
            raw = raw * (2.0 * NORM) / (reach * reach * reach)
            density = jnp.where(lane < count_ref[cell], raw, 1.0)
            density_ref[line, :] = density
            factor_ref[line, :] = 2.0 / 3.0 * heat_ref[line, :] / density
        return carry

    lax.fori_loop(0, CELLS // 4, some_cells, 0)

    def one_peer(peer, carry):
        cells = [jnp.maximum(export_ref[peer, slot], 0) for slot in range(CAP)]
        sent_ref[receiver(peer, me_ref[0], sent_ref.shape[0])] = jnp.concatenate(
            [factor_ref[pl.ds(cell, 1), :] for cell in cells], axis=0
        )
        return carry

    lax.fori_loop(0, 2 * HALF, one_peer, 0)


def far_self_kernel(own_ref, factor_ref, table_ref, total_ref, *refs):
    total_ref[...] = jnp.zeros_like(total_ref)

    def pair(cell):
        return cell, cell, own_ref[cell], NO_SHIFT, factor_ref[pl.ds(cell, 1), :]

    far_pairs(0, CELLS, table_ref, total_ref, refs, pair)


def far_cross_kernel(
    count_ref,
    info_ref,
    shift_ref,
    table_ref,
    own_ref,
    far_a_ref,
    far_b_ref,
    far_factor_ref,
    factor_ref,
    near_ref,
    before_ref,
    push_ref,
    total_ref,
    list_ref,
    *refs,
):
    total_ref[...] = before_ref[...]
    for which, far_ref in enumerate((far_a_ref, far_b_ref)):
        amount = listed(which, info_ref, list_ref)

        def pair(place, far_ref=far_ref):
            owner, target, source, shift = pair_at(list_ref, info_ref, shift_ref, place)
            line = info_ref[3, jnp.minimum(list_ref[place], info_ref.shape[1] - 1)]
            return owner, target, far_ref[source], shift, far_factor_ref[pl.ds(line, 1), :]

        far_pairs(0, amount, table_ref, total_ref, refs, pair)

    lane = lax.broadcasted_iota(jnp.int32, (1, SLOTS), 1)

    def some_cells(step, carry):
        for part in range(4):
            cell = step * 4 + part
            own = -(near_ref[cell, 0:8, :] + near_ref[cell, 8:16, :])
            far = total_ref[cell, 0:8, :] + total_ref[cell, 8:16, :]
            block = own_ref[cell]
            _, place = place_rows(block, NO_SHIFT)
            reach = block[7:8]
            inverse = 1.0 / (reach * reach)
            scale = factor_ref[pl.ds(cell, 1), :] * (6.0 * NORM) * inverse * inverse / reach
            place = place[0:3]
            speed = block[4:7]
            push = scale * (own[0:3] - place * own[3:4]) + (far[0:3] - place * far[3:4])
            warm = jnp.sum(
                speed * place * own[3:4] - speed * own[0:3] - place * own[4:7],
                axis=0,
                keepdims=True,
            )
            warm = scale * (warm + own[7:8])
            live = lane < count_ref[cell]
            push = jnp.where(live, push, 0.0)
            for line in range(3):
                push_ref[line, pl.ds(cell, 1), :] = push[line : line + 1]
            push_ref[3, pl.ds(cell, 1), :] = jnp.where(live, warm, 0.0)
        return carry

    lax.fori_loop(0, CELLS // 4, some_cells, 0)


def receiver(peer, me, devices):
    step = jnp.where(peer < HALF, peer - HALF, peer - HALF + 1)
    return lax.rem(me - step + devices, devices)


def export_kernel(
    devices,
    me_ref,
    export_ref,
    count_ref,
    place_ref,
    speed_ref,
    mass_ref,
    reach_ref,
    own_ref,
    live_ref,
    sent_a_ref,
    sent_b_ref,
):
    lane = lax.broadcasted_iota(jnp.int32, (1, SLOTS), 1)

    def some_cells(step, carry):
        for part in range(4):
            cell = step * 4 + part
            line = pl.ds(cell, 1)
            lanes = pl.ds(pl.multiple_of(cell * SLOTS, SLOTS), SLOTS)
            mass = jnp.where(lane < count_ref[cell], mass_ref[line, :], 0.0)
            live_ref[line, :] = mass
            own_ref[cell] = jnp.concatenate(
                [place_ref[:, lanes], mass / SLOTS, speed_ref[:, lanes], reach_ref[line, :]], axis=0
            )
        return carry

    lax.fori_loop(0, CELLS // 4, some_cells, 0)
    me = me_ref[0]

    def one_peer(peer, carry):
        target = receiver(peer, me, devices)
        same = target // GROUP == me // GROUP
        seat_a = lax.rem(target, GROUP) * CAP
        seat_b = lax.rem(target + devices - GROUP // 2, GROUP) * CAP

        @pl.when(same)
        def _():
            for slot in range(CAP):
                sent_a_ref[seat_a + slot] = own_ref[jnp.maximum(export_ref[peer, slot], 0)]

        @pl.when(jnp.logical_not(same))
        def _():
            for slot in range(CAP):
                sent_b_ref[seat_b + slot] = own_ref[jnp.maximum(export_ref[peer, slot], 0)]

        return carry

    lax.fori_loop(0, 2 * HALF, one_peer, 0)


def sort_kernel(owner_ref, cell_ref, mass_ref, mass_out, cell_out, parts_ref):
    span = 256
    together = 4
    devices = 128
    device_row = row_index((devices, span))
    slot_row = device_row.astype(F32)
    before = (
        row_index((span, span)) <= lax.broadcasted_iota(jnp.int32, (span, span), 1)
    ).astype(F32).astype(BF16)
    parts_ref[...] = jnp.zeros_like(parts_ref)

    def chunk(step, taken):
        named, values = [], []
        for part in range(together):
            line = pl.ds(step * together + part, 1)
            cell = cell_ref[line, :]
            chosen = device_row == owner_ref[line, :]
            ones = chosen.astype(F32)
            upto = lax.dot_general(ones.astype(BF16), before, NN, preferred_element_type=F32)
            rank = jnp.sum(ones * (upto + taken), axis=0, keepdims=True) - 1.0
            taken = taken + upto[:, span - 1 : span]
            named.append((slot_row == rank).astype(F32).astype(BF16))
            parts = thirds(mass_ref[line, :]) + (
                (cell & 63).astype(F32),
                ((cell >> 6) & 63).astype(F32),
                (cell >> 12).astype(F32),
            )
            values.append(
                jnp.concatenate([jnp.where(chosen, item, 0.0) for item in parts], axis=0).astype(BF16)
            )
        parts_ref[...] += lax.dot_general(
            jnp.concatenate(values, axis=1),
            jnp.concatenate(named, axis=1),
            NT,
            preferred_element_type=F32,
        )
        return taken

    lax.fori_loop(0, owner_ref.shape[0] // together, chunk, jnp.zeros((devices, 1), F32))
    n = devices
    mass_out[...] = (parts_ref[0:n] + parts_ref[n : 2 * n]) + parts_ref[2 * n : 3 * n]
    cell_out[...] = (
        parts_ref[3 * n : 4 * n]
        + 64.0 * parts_ref[4 * n : 5 * n]
        + 4096.0 * parts_ref[5 * n : 6 * n]
    )


def put_line(ref, line, rows):
    ref[pl.Slice(line, 128, 16), :] = rows[:, 0:128]
    ref[pl.Slice(8 + line, 128, 16), :] = rows[:, 128:256]


def get_line(ref, line):
    return jnp.concatenate(
        [ref[pl.Slice(line, 128, 16), :], ref[pl.Slice(8 + line, 128, 16), :]], axis=1
    )


def dot32(left, right):
    return lax.dot_general(left, right, NN, precision=highest, preferred_element_type=F32)


def dot_halves(left, right):
    left_high, left_low = split(left)
    right_high, right_low = split(right)
    return lax.dot_general(
        jnp.concatenate([left_high, left_high, left_low], axis=1),
        jnp.concatenate([right_high, right_low, right_high], axis=0),
        NN,
        preferred_element_type=F32,
    )


def deposit_kernel(mass_ref, cell_ref, z_ref, y_ref, out_ref, grid_ref):
    lanes = 128
    planes = grid_ref.shape[0]
    rows_at = row_index((planes, lanes))
    deep_at = row_index((M, lanes))
    grid_ref[...] = jnp.zeros_like(grid_ref)
    group = 8

    def chunk(step, carry):
        left, first, second = [], [], []
        for part in range(group):
            cell = cell_ref[pl.ds(step * group + part, 1), :].astype(jnp.int32)
            mass = mass_ref[pl.ds(step * group + part, 1), :]
            high = rounded(mass)
            low = mass - high
            left.append((rows_at == (cell >> 8)).astype(F32).astype(BF16))
            named = deep_at == (cell & 255)
            first.append(jnp.where(named, high, 0.0).astype(BF16))
            second.append(jnp.where(named, low, 0.0).astype(BF16))
        left = jnp.concatenate(left + left, axis=1)
        right = jnp.concatenate(first + second, axis=1)
        grid_ref[...] += lax.dot_general(left, right, NT, preferred_element_type=F32)
        return carry

    lax.fori_loop(0, mass_ref.shape[0] // group, chunk, 0)
    for plane in range(planes // M):
        piece = grid_ref[plane * M : (plane + 1) * M, :]
        turned = jnp.concatenate(
            [dot32(piece, z_ref[:, 0:M]), dot32(piece, z_ref[:, M : 2 * M])], axis=0
        )
        for part in range(4):
            rows = dot32(y_ref[part * 128 : (part + 1) * 128, :], turned)
            put_line(out_ref, plane * 4 + part, rows)


def filter_kernel(first_ref, in_ref, forward_ref, back_ref, out_ref):
    for line in range(2):
        pieces = [
            get_line(in_ref, plane * 4 + part * 2 + line)
            for part in range(2)
            for plane in range(2)
        ]
        spectrum = dot32(forward_ref[...], jnp.concatenate(pieces, axis=0))
        along_x = row_index((M, M))
        along_z = lax.broadcasted_iota(jnp.int32, (M, M), 1)
        along_x = jnp.where(along_x < M // 2, along_x, along_x - M)
        along_z = jnp.where(along_z < M // 2, along_z, along_z - M)
        along_y = first_ref[0] + line
        along_y = jnp.where(along_y < M // 2, along_y, along_y - M)
        square = (along_x * along_x + along_z * along_z + along_y * along_y).astype(F32)
        step = 2.0 * math.pi / M
        green = jnp.where(square > 0, -1.0 / (step * step * jnp.maximum(square, 1.0)), 0.0)
        spectrum = jnp.concatenate([spectrum[0:M] * green, spectrum[M : 2 * M] * green], axis=0)
        result = dot32(back_ref[...], spectrum)
        for piece in range(4):
            part, plane = piece // 2, piece % 2
            put_line(
                out_ref, plane * 4 + part * 2 + line, result[piece * 128 : (piece + 1) * 128]
            )


def potential_kernel(in_ref, y_ref, z_ref, out_ref):
    for plane in range(2):
        pieces = [get_line(in_ref, plane * 4 + part) for part in range(4)]
        turned = dot_halves(y_ref[...], jnp.concatenate(pieces, axis=0))
        out_ref[plane] = dot_halves(
            jnp.concatenate([turned[0:M], turned[M : 2 * M]], axis=1), z_ref[...]
        )


def wave_tables():
    index = np.arange(M)
    angle = 2.0 * np.pi / M * (np.outer(index, index) % M)
    cosine, sine = np.cos(angle), np.sin(angle)
    pairs = np.concatenate([index[0::2], index[1::2]])
    z_forward = np.concatenate([cosine, -sine], axis=1)
    y_forward = np.block([[cosine[pairs], sine[pairs]], [-sine[pairs], cosine[pairs]]])
    x_forward = np.block([[cosine[:, pairs], sine[:, pairs]], [-sine[:, pairs], cosine[:, pairs]]])
    x_back = np.block([[cosine[pairs], -sine[pairs]], [sine[pairs], cosine[pairs]]])
    y_back = np.block([[cosine[:, pairs], -sine[:, pairs]], [sine[:, pairs], cosine[:, pairs]]])
    z_back = np.concatenate([cosine, -sine], axis=0) / float(M) ** 3
    return [
        np.asarray(item, np.float32)
        for item in (z_forward, y_forward, x_forward, x_back, y_back, z_back)
    ]


def per_device(
    positions,
    velocities,
    masses,
    smoothing,
    energies,
    cell_counts,
    pair_list,
    export_list,
    mesh_owner,
    mesh_cell,
):
    devices = lax.axis_size("cells")
    me = lax.axis_index("cells").astype(jnp.int32)
    heat = energies.reshape(CELLS, SLOTS)

    groups_a = [list(range(g, g + GROUP)) for g in range(0, devices, GROUP)]
    groups_b = [[(i + GROUP // 2) % devices for i in g] for g in groups_a]
    def swap(data, groups):
        return lax.all_to_all(data, "cells", 0, 0, axis_index_groups=groups, tiled=True)

    def after(data, *others):
        return lax.optimization_barrier((data, *others))[0]

    exports = export_list[0]
    here = me.reshape(1)
    sent = jax.ShapeDtypeStruct((GROUP * CAP, 8, SLOTS), F32)
    own, mass, sent_a, sent_b = pl.pallas_call(
        functools.partial(export_kernel, devices),
        out_shape=[
            jax.ShapeDtypeStruct((CELLS, 8, SLOTS), F32),
            jax.ShapeDtypeStruct((CELLS, SLOTS), F32),
            sent,
            sent,
        ],
        in_specs=[SMEM] * 3 + [VMEM] * 4,
        out_specs=[VMEM] * 4,
        compiler_params=params(32),
        cost_estimate=cost(2e9, 5e6),
        name="exports",
    )(
        here,
        exports,
        cell_counts,
        positions,
        velocities,
        masses.reshape(CELLS, SLOTS),
        smoothing.reshape(CELLS, SLOTS),
    )
    far_a = swap(sent_a, groups_a)
    mesh_owner, mesh_cell, mass = lax.optimization_barrier((mesh_owner, mesh_cell, mass, sent_a))[:3]

    owner_cell, neighbour, slot, direction = (pair_list[i] for i in range(4))
    step = jnp.where(neighbour < HALF, neighbour - HALF, neighbour - HALF + 1)
    other = (me + step) % devices
    in_a = other // GROUP == me // GROUP
    place = jnp.where(in_a, other % GROUP, (other - GROUP // 2) % GROUP)
    info = jnp.stack(
        [owner_cell, place * CAP + slot, jnp.where(in_a, 0, 1), other * CAP + slot]
    ).astype(jnp.int32)
    shift = jnp.stack([direction // 9 - 1, direction // 3 % 3 - 1, direction % 3 - 1]).astype(F32)

    lines = CELLS * SLOTS // 256
    mass_sent, cell_sent = pl.pallas_call(
        sort_kernel,
        out_shape=[jax.ShapeDtypeStruct((devices, 128), F32)] * 2,
        in_specs=[VMEM] * 3,
        out_specs=[VMEM] * 2,
        scratch_shapes=[pltpu.VMEM((6 * 128, 128), F32)],
        compiler_params=params(32),
        cost_estimate=cost(6e9, 1e6),
        name="sort_masses",
    )(mesh_owner.reshape(lines, 256), mesh_cell.reshape(lines, 256), mass.reshape(lines, 256))

    near_sums = jax.ShapeDtypeStruct((CELLS + 1, 32, SLOTS), F32)
    far_sums = jax.ShapeDtypeStruct((CELLS + 1, 16, SLOTS), F32)
    features = jax.ShapeDtypeStruct((CELLS, 48, SLOTS), BF16)
    each = jax.ShapeDtypeStruct((CELLS, SLOTS), F32)
    places = [pltpu.SMEM((256,), jnp.int32)]
    scaled, table, near = pl.pallas_call(
        near_self_kernel,
        out_shape=[features, features, near_sums],
        in_specs=[VMEM],
        out_specs=[VMEM] * 3,
        scratch_shapes=pair_scratch(4),
        compiler_params=params(48),
        cost_estimate=cost(8e9, 1e6),
        name="near_self",
    )(own)

    swapped = swap(after(jnp.stack([mass_sent, cell_sent], axis=1), far_a, near), None)
    far_b = swap(after(sent_b, swapped), groups_b)

    near = pl.pallas_call(
        near_early_kernel,
        out_shape=near_sums,
        in_specs=[SMEM] * 2 + [VMEM] * 3,
        out_specs=VMEM,
        scratch_shapes=places + pair_scratch(4),
        compiler_params=params(48),
        cost_estimate=cost(1.5e10, 1e6),
        name="near_early",
    )(info, shift, scaled, far_a, near)
    z_forward, y_forward, x_forward, x_back, y_back, z_back = wave_tables()
    wide = jax.ShapeDtypeStruct((devices * 16, M // 2), F32)
    half_way = pl.pallas_call(
        deposit_kernel,
        out_shape=wide,
        in_specs=[VMEM] * 4,
        out_specs=VMEM,
        scratch_shapes=[pltpu.VMEM((2 * M, M), F32)],
        compiler_params=params(48),
        cost_estimate=cost(1.5e10, 1e6),
        name="deposit",
    )(swapped[:, 0], swapped[:, 1], z_forward, y_forward)
    half_way = swap(after(half_way.reshape(devices, 16, M // 2), far_b, near), None)
    near, density, factor, sent_factor = pl.pallas_call(
        near_late_kernel,
        out_shape=[near_sums, each, each, jax.ShapeDtypeStruct((devices, CAP, SLOTS), F32)],
        in_specs=[SMEM] * 5 + [VMEM] * 6,
        out_specs=[VMEM] * 4,
        scratch_shapes=places + pair_scratch(4),
        compiler_params=params(48),
        cost_estimate=cost(1.5e10, 1e6),
        name="near_late",
    )(here, exports, cell_counts, info, shift, scaled, far_a, far_b, near, own, heat)
    far_factor = swap(after(sent_factor, half_way), None).reshape(devices * CAP, SLOTS)

    far_total = pl.pallas_call(
        far_self_kernel,
        out_shape=far_sums,
        in_specs=[VMEM] * 3,
        out_specs=VMEM,
        scratch_shapes=pair_scratch(2),
        compiler_params=params(48),
        cost_estimate=cost(8e9, 1e6),
        name="far_self",
    )(own, factor, table)
    push = pl.pallas_call(
        far_cross_kernel,
        out_shape=jax.ShapeDtypeStruct((4, CELLS, SLOTS), F32),
        in_specs=[SMEM] * 3 + [VMEM] * 8,
        out_specs=VMEM,
        scratch_shapes=[pltpu.VMEM(far_sums.shape, F32)] + places + pair_scratch(2),
        compiler_params=params(48),
        cost_estimate=cost(3e10, 1e6),
        name="far_cross",
    )(cell_counts, info, shift, table, own, far_a, far_b, far_factor, factor, near, far_total)
    acceleration = push[0:3].reshape(3, -1)
    heating = push[3].reshape(-1)

    back = pl.pallas_call(
        filter_kernel,
        out_shape=wide,
        in_specs=[SMEM] + [VMEM] * 3,
        out_specs=VMEM,
        compiler_params=params(48),
        cost_estimate=cost(5e9, 1e6),
        name="filter",
    )((2 * me).reshape(1), half_way.reshape(devices * 16, M // 2), x_forward, x_back)
    back = swap(after(back.reshape(devices, 16, M // 2), far_factor, far_total), None)
    potential = pl.pallas_call(
        potential_kernel,
        out_shape=jax.ShapeDtypeStruct((2, M, M), F32),
        in_specs=[VMEM] * 3,
        out_specs=VMEM,
        compiler_params=params(48),
        cost_estimate=cost(4e9, 1e6),
        name="potential",
    )(back.reshape(devices * 16, M // 2), y_back, z_back)
    return (density.reshape(-1), acceleration, heating, potential)


def solution(mesh):
    in_specs = (
        P(None, "cells"),
        P(None, "cells"),
        P("cells"),
        P("cells"),
        P("cells"),
        P("cells"),
        P(None, "cells"),
        P("cells", None, None),
        P("cells", None),
        P("cells"),
    )
    out_specs = (P("cells"), P(None, "cells"), P("cells"), P("cells", None, None))
    return jax.shard_map(
        per_device, mesh=mesh, in_specs=in_specs, out_specs=out_specs, check_vma=False
    )
```
